128 devices in a mesh: section: 8 (over x, y_lo), dp: 16 (over y_hi, z, core).
Axes of the slice: x: 4, y: 4 (y_hi: 2, y_lo: 2; y = y_hi * 2 + y_lo), z: 4, core: 2. Of those that a mesh axis runs over, the one named last changes fastest.
Arguments:
- hidden_in: bfloat16 [8, 16, 256, 2048], P('section', 'dp'), may hold values from -6 to 6
- grad_out: bfloat16 [16, 256, 2048], P('dp'), may hold values from -6 to 6
- encoder_out: bfloat16 [16, 256, 2048], P('dp', 'section'), may hold values from -6 to 6
- enc_valid: int32 [16, 256], P('dp', 'section'), may hold values from 0 to 1, as said below
- norm_gain: bfloat16 [8, 2048], P('section'), may hold values from 0.099609375 to 1.8984375
- w_query: bfloat16 [8, 2048, 2048], P('section', 'dp'), may hold values from -0.015625 to 0.015625
- w_key: bfloat16 [8, 2048, 2048], P('section', 'dp'), may hold values from -0.125 to 0.125
- w_value: bfloat16 [8, 2048, 2048], P('section', 'dp'), may hold values from -0.125 to 0.125
- w_out: bfloat16 [8, 2048, 2048], P('section', 'dp'), may hold values from -0.875 to 0.875
Outputs:
- grad_in: bfloat16 [8, 16, 256, 2048], P('section', 'dp')
- grad_encoder: bfloat16 [16, 256, 2048], P('dp', 'section')
The draws below stay inside these ranges and needn't reach their ends.
Inputs may be any that keep to these rules, and one draw needn't show every extreme that they name: `enc_valid`: each row is 1 on a prefix of 128 or more positions and 0 after it.
All inputs are finite; a program needn't handle non-finite values.
Results may differ from the reference program's by a relative error of at most 0.04.
Values may be sent and summed in bfloat16 or wider, within the bound.
A program may use at most 192 MiB of HBM per device.

```python
import jax
import jax.numpy as jnp
from jax import lax

D = 2048
HEAD = 64
DEC_LEN = 256
ENC_LEN = 256
INNER = 2048
SEQS = 16
SECTIONS = 8


def draw_enc_valid(key, part):
    lengths = jax.random.randint(key, (SEQS,), ENC_LEN // 2, ENC_LEN + 1)
    lengths = lengths.at[0].set(ENC_LEN // 2).at[SEQS - 1].set(ENC_LEN)
    positions = jnp.arange(ENC_LEN, dtype=jnp.int32)
    return (positions[None, :] < lengths[:, None]).astype(jnp.int32)


def shard_levels(key, extent, cuts, smallest, high):
    def one(axis_at, shards_of):
        steps = jax.random.uniform(jax.random.fold_in(jax.random.fold_in(key, 6), axis_at), (shards_of,), jnp.float32, smallest / len(cuts), high / len(cuts))
        return jnp.repeat(jnp.exp(steps), extent[axis_at] // shards_of).reshape((-1,) + (1,) * (len(extent) - axis_at - 1))

    gain = one(*cuts[0])
    for cut in cuts[1:]:
        gain = gain * one(*cut)
    return gain


def normal_values(own_key, dims, deviation, bound, shards=(), held_as=jnp.bfloat16):
    array = deviation * jax.random.normal(own_key, dims, jnp.float32)
    if shards:
        array = array * shard_levels(own_key, dims, shards, -0.22, 0.18)
    return jnp.clip(array, -bound, bound).astype(held_as)


def setup_inputs(seed: int = 0) -> dict:
    arg_keys = jax.random.split(jax.random.key(seed), 10)
    hidden_in = normal_values(arg_keys[0], (SECTIONS, SEQS, DEC_LEN, D), 1.0, 6.0, ((0, 8), (1, 16)))
    grad_out = normal_values(arg_keys[1], (SEQS, DEC_LEN, D), 1.0, 6.0, ((0, 16),))
    encoder_out = normal_values(arg_keys[2], (SEQS, ENC_LEN, D), 1.0, 6.0, ((0, 16), (1, 8)))
    enc_valid = draw_enc_valid(jax.random.fold_in(arg_keys[9], 71), 0)
    norm_gain = jnp.clip(1.0 + 0.18 * jax.random.normal(arg_keys[4], (SECTIONS, D), jnp.float32), 0.099609375, 1.8984375).astype(jnp.bfloat16)
    w_query = normal_values(arg_keys[5], (SECTIONS, D, INNER), (D * HEAD) ** -0.5, 0.015625, ((0, 8), (1, 16)))
    w_key = normal_values(arg_keys[6], (SECTIONS, D, INNER), D ** -0.5, 0.125, ((0, 8), (1, 16)))
    w_value = normal_values(arg_keys[7], (SECTIONS, D, INNER), D ** -0.5, 0.125, ((0, 8), (1, 16)))
    w_out = normal_values(arg_keys[8], (SECTIONS, INNER, D), (6 * INNER // ENC_LEN) ** -0.5, 0.875, ((0, 8), (1, 16)))
    return dict(hidden_in=hidden_in, grad_out=grad_out, encoder_out=encoder_out, enc_valid=enc_valid, norm_gain=norm_gain, w_query=w_query, w_key=w_key, w_value=w_value, w_out=w_out)


def forward_section(inputs, gain_row, query_weight, key_weight, value_weight, encoded, valid_keys):
    seq_count, dec_rows, width = inputs.shape
    enc_rows = encoded.shape[1]
    inner_width = query_weight.shape[1]
    head_count = inner_width // HEAD
    in_float = inputs.astype(jnp.float32)
    inv_rms = lax.rsqrt(lax.optimization_barrier(jnp.mean(in_float * in_float, axis=2, keepdims=True)) + 1e-06)
    normed = (in_float * inv_rms * gain_row.astype(jnp.float32)).astype(jnp.bfloat16)
    queries = jnp.dot(normed.reshape(-1, width), query_weight, preferred_element_type=jnp.float32).astype(jnp.bfloat16)
    queries = queries.reshape(seq_count, dec_rows, head_count, HEAD)
    keys_all = jnp.dot(encoded.reshape(-1, width), key_weight, preferred_element_type=jnp.float32).astype(jnp.bfloat16)
    keys_all = keys_all.reshape(seq_count, enc_rows, head_count, HEAD)
    values_all = jnp.dot(encoded.reshape(-1, width), value_weight, preferred_element_type=jnp.float32).astype(jnp.bfloat16)
    values_all = values_all.reshape(seq_count, enc_rows, head_count, HEAD)
    scores = jnp.einsum('slhd,sehd->shle', queries.astype(jnp.float32), keys_all.astype(jnp.float32))
    raw = jnp.exp(scores) * valid_keys.astype(jnp.float32)[:, None, None, :]
    attn_prob = raw / lax.optimization_barrier(jnp.sum(raw, axis=3, keepdims=True))
    return (in_float, inv_rms, queries, keys_all, values_all, attn_prob)

def backward_section(grad_y, saved, gain_row, query_weight, out_weight):
    in_float, inv_rms, queries, keys_all, values_all, attn_prob = saved
    seq_count, dec_rows, width = grad_y.shape
    head_count = queries.shape[2]
    enc_rows = keys_all.shape[1]
    grad_attn = jnp.dot(grad_y.reshape(-1, width), out_weight.T, preferred_element_type=jnp.float32).astype(jnp.bfloat16)
    grad_attn = grad_attn.reshape(seq_count, dec_rows, head_count, HEAD)
    grad_prob = jnp.einsum('slhd,sehd->shle', grad_attn.astype(jnp.float32), values_all.astype(jnp.float32))
    inner_sum = lax.optimization_barrier(jnp.sum(attn_prob * grad_prob, axis=3, keepdims=True))
    grad_scores = (attn_prob * (grad_prob - inner_sum)).astype(jnp.bfloat16)
    prob_half = attn_prob.astype(jnp.bfloat16)
    grad_query = jnp.einsum('shle,sehd->slhd', grad_scores.astype(jnp.float32), keys_all.astype(jnp.float32)).astype(jnp.bfloat16)
    grad_key = jnp.einsum('shle,slhd->sehd', grad_scores.astype(jnp.float32), queries.astype(jnp.float32)).astype(jnp.bfloat16)
    grad_value = jnp.einsum('shle,slhd->sehd', prob_half.astype(jnp.float32), grad_attn.astype(jnp.float32)).astype(jnp.bfloat16)
    grad_normed = jnp.dot(grad_query.reshape(seq_count * dec_rows, -1), query_weight.T, preferred_element_type=jnp.float32)
    grad_normed = grad_normed.reshape(seq_count, dec_rows, width)
    scaled_grad = gain_row.astype(jnp.float32) * grad_normed
    branch = inv_rms * scaled_grad - in_float * inv_rms * inv_rms * inv_rms * lax.optimization_barrier(jnp.mean(in_float * scaled_grad, axis=2, keepdims=True))
    grad_input = (grad_y.astype(jnp.float32) + branch).astype(jnp.bfloat16)
    return (grad_input, grad_key.reshape(seq_count * enc_rows, -1), grad_value.reshape(seq_count * enc_rows, -1))

def reference(hidden_in, grad_out, encoder_out, enc_valid, norm_gain, w_query, w_key, w_value, w_out):
    grad_now = grad_out
    grad_list = []
    enc_total = jnp.zeros((SEQS * ENC_LEN, D), jnp.float32)
    for section_index in reversed(range(SECTIONS)):
        saved = forward_section(hidden_in[section_index], norm_gain[section_index], w_query[section_index], w_key[section_index], w_value[section_index], encoder_out, enc_valid)
        grad_now, grad_key, grad_value = backward_section(grad_now, saved, norm_gain[section_index], w_query[section_index], w_out[section_index])
        grad_list.insert(0, grad_now)
        enc_total = enc_total + jnp.dot(grad_key, w_key[section_index].T, preferred_element_type=jnp.float32)
        enc_total = enc_total + jnp.dot(grad_value, w_value[section_index].T, preferred_element_type=jnp.float32)
    grad_encoder = enc_total.reshape(SEQS, ENC_LEN, D).astype(jnp.bfloat16)
    return (jnp.stack(grad_list), grad_encoder)
```

```python
import functools

import jax
import jax.numpy as jnp
from jax import lax
from jax.experimental import pallas as pl
from jax.experimental.pallas import tpu as pltpu
from jax.sharding import PartitionSpec as P

HEAD = 64
MESH = pl.DeviceIdType.MESH
F32 = jnp.float32
BF16 = jnp.bfloat16

FULL = 2048
HALF = FULL // 2
PART_A = 1152
HALF_A = PART_A // 2
COPIES = 27
CHUNK = 32


def copy_plan():
    part_b = FULL - PART_A
    return [
        (0, 0, 0, FULL, "z+"),
        (0, 0, 0, FULL, "z-"),
        (0, 0, 0, PART_A, "y"),
        (0, 0, PART_A, part_b, "y"),
        (0, 0, 0, FULL, "core"),
        (0, -1, 0, HALF, "z+"),
        (0, -1, PART_A, part_b, "y"),
        (0, -1, 0, FULL, "core"),
        (0, 1, HALF, HALF, "z-"),
        (0, 1, PART_A, part_b, "y"),
        (0, 1, 0, FULL, "core"),
        (1, 0, 0, PART_A, "z+"),
        (1, 0, 0, PART_A, "z-"),
        (1, 0, 0, PART_A, "core"),
        (1, 0, PART_A, part_b, "core"),
        (0, 2, 0, HALF, "core"),
        (0, 2, PART_A, part_b, "y"),
        (0, 2, HALF, HALF, "core"),
        (1, -1, 0, HALF_A, "z+"),
        (1, -1, 0, PART_A, "core"),
        (1, 1, HALF_A, HALF_A, "z-"),
        (1, 1, 0, PART_A, "core"),
        (1, -1, PART_A, part_b, "core"),
        (1, 1, PART_A, part_b, "core"),
        (1, 2, 0, HALF_A, "core"),
        (1, 2, HALF_A, HALF_A, "core"),
        (1, 2, PART_A, part_b, "core"),
    ]


PLAN = copy_plan()
STAGES = [
    ((), (0, 1, 2, 3, 4)),
    ((0, 1, 2, 3), (5, 8, 11, 12, 6, 9, 7, 10, 13, 14)),
    ((5, 8, 11, 12, 6, 9), (18, 20, 16, 15, 17, 19, 21, 22, 23)),
    ((18, 20, 16), (24, 25, 26)),
    ((4, 7, 10, 13, 14, 15, 17, 19, 21, 22, 23, 24, 25, 26), ()),
]


class Gather:
    def __init__(self, own_ref, full_ref, send_sem, recv_sem, local_sem):
        self.own, self.full = own_ref, full_ref
        self.send_sem, self.recv_sem, self.local_sem = send_sem, recv_sem, local_sem
        self.section, dp = lax.axis_index("section"), lax.axis_index("dp")
        self.half, self.z, self.core = dp // 8, (dp // 2) % 4, dp % 2

    def dp_of(self, half, z, core):
        return half * 8 + ((z + 4) % 4) * 2 + core

    def target(self, name):
        half, z, core = self.half, self.z, self.core
        dp = {
            "z+": self.dp_of(half, z + 1, core),
            "z-": self.dp_of(half, z + 3, core),
            "y": self.dp_of(1 - half, z, core),
            "core": self.dp_of(half, z, 1 - core),
        }[name]
        return (self.section, dp)

    def greet(self, barrier):
        for name in ("z+", "z-", "y", "core"):
            pl.semaphore_signal(barrier, inc=1, device_id=self.target(name), device_id_type=MESH)
        return 4

    def copy(self, matrix, k):
        half_off, z_off, first, rows, name = PLAN[k]
        half = 1 - self.half if half_off else self.half
        unit = self.dp_of(half, self.z + (z_off + 4) % 4, self.core)
        dst = self.full.at[matrix, unit, pl.ds(first, rows)]
        own = half_off == 0 and z_off == 0
        src = self.own.at[matrix, pl.ds(first, rows)] if own else dst
        return pltpu.make_async_remote_copy(
            src_ref=src,
            dst_ref=dst,
            send_sem=self.send_sem.at[matrix, k],
            recv_sem=self.recv_sem.at[matrix, k],
            device_id=self.target(name),
            device_id_type=MESH,
        )

    def arrival(self, matrix, k):
        return self.copy(matrix, k)

    def local(self, matrix):
        me = self.dp_of(self.half, self.z, self.core)
        return pltpu.make_async_copy(
            self.own.at[matrix], self.full.at[matrix, me], self.local_sem.at[matrix]
        )

    def stage(self, matrix, number):
        waits, starts = STAGES[number]
        if number == 0:
            self.local(matrix).start()
        for k in waits:
            self.arrival(matrix, k).wait_recv()
        for k in starts:
            self.copy(matrix, k).start()

    def finish(self, matrix):
        self.local(matrix).wait()
        for k in range(COPIES):
            self.copy(matrix, k).wait_send()


def gather_kernel(own_ref, full_ref, send_sem, recv_sem, local_sem):
    gather = Gather(own_ref, full_ref, send_sem, recv_sem, local_sem)
    barrier = pltpu.get_barrier_semaphore()
    pl.semaphore_wait(barrier, gather.greet(barrier))
    matrices, stages = 4, len(STAGES)
    for step in range(matrices + stages - 1):
        for number in range(stages):
            matrix = step - number
            if 0 <= matrix < matrices:
                gather.stage(matrix, number)
    for matrix in range(matrices):
        gather.finish(matrix)


def gather_weights(own):
    return pl.pallas_call(
        gather_kernel,
        out_shape=jax.ShapeDtypeStruct((4, 16, FULL, 128), BF16),
        in_specs=[pl.BlockSpec(memory_space=pl.ANY)],
        out_specs=pl.BlockSpec(memory_space=pl.ANY),
        scratch_shapes=[
            pltpu.SemaphoreType.DMA((4, COPIES)),
            pltpu.SemaphoreType.DMA((4, COPIES)),
            pltpu.SemaphoreType.DMA((4,)),
        ],
        compiler_params=pltpu.CompilerParams(collective_id=0, has_side_effects=True),
    )(own)


def wide(ref, first, count):
    return jnp.concatenate([ref[first + i] for i in range(count)], axis=1)


def relay_chunk(rows, gy_ref, x_ref, gain_ref, wo_ref, wq_ref, k_ref, vt_ref, p_ref, ga_ref, gs_ref, gq_ref, gn_ref, out_ref):
    count = CHUNK
    width = FULL
    grad_y = gy_ref[rows, :]
    for j in range(2):
        part = jnp.dot(grad_y, wide(wo_ref, 8 * j, 8), preferred_element_type=F32)
        ga_ref[rows, j * 1024 : (j + 1) * 1024] = part.astype(BF16)
    low = lax.broadcasted_iota(jnp.int32, (count, 128), 1) < HEAD
    zero = jnp.zeros((count, 128), BF16)
    for pair in range(16):
        lanes = slice(pair * 128, (pair + 1) * 128)
        ga = ga_ref[rows, lanes]
        both = jnp.concatenate([jnp.where(low, ga, zero), jnp.where(low, zero, ga)], axis=0)
        grad_prob = jnp.dot(both, vt_ref[lanes, :], preferred_element_type=F32)
        prob = jnp.concatenate([p_ref[2 * pair, rows, :], p_ref[2 * pair + 1, rows, :]], axis=0)
        prob = prob.astype(F32)
        inner = jnp.sum(prob * grad_prob, axis=1, keepdims=True)
        grad_scores = (prob * (grad_prob - inner)).astype(BF16)
        gs_ref[2 * pair, rows, :] = grad_scores[:count]
        gs_ref[2 * pair + 1, rows, :] = grad_scores[count:]
        grad_query = jnp.dot(grad_scores, k_ref[:, lanes], preferred_element_type=F32)
        gq_ref[:, lanes] = jnp.where(low, grad_query[:count], grad_query[count:]).astype(BF16)
    grad_query = gq_ref[...]
    for j in range(2):
        gn_ref[:, j * 1024 : (j + 1) * 1024] = jnp.dot(
            grad_query, wide(wq_ref, 8 * j, 8), preferred_element_type=F32
        )
    x = x_ref[rows, :].astype(F32)
    inv_rms = lax.rsqrt(jnp.sum(x * x, axis=1, keepdims=True) * (1.0 / width) + 1e-06)
    scaled = gn_ref[...] * gain_ref[...].astype(F32)
    mean = jnp.sum(x * scaled, axis=1, keepdims=True) * (1.0 / width)
    branch = inv_rms * scaled - x * (inv_rms * inv_rms * inv_rms * mean)
    out_ref[rows, :] = (grad_y.astype(F32) + branch).astype(BF16)


def relay_kernel(
    gout_ref, x_ref, gain_ref, wo_ref, wq_ref, k_ref, vt_ref, p_ref,
    out_ref, ga_ref, gs_ref,
    gy_ref, gq_ref, gn_ref, send_sem, recv_sem,
):
    sections = lax.axis_size("section")
    section, dp = lax.axis_index("section"), lax.axis_index("dp")
    before, after = (section + sections - 1) % sections, (section + 1) % sections
    barrier = pltpu.get_barrier_semaphore()
    for other in (before, after):
        pl.semaphore_signal(barrier, inc=1, device_id=(other, dp), device_id_type=MESH)
    pl.semaphore_wait(barrier, 2)

    @pl.when(section == sections - 1)
    def _():
        gy_ref[...] = gout_ref[...]

    chunks = gy_ref.shape[0] // CHUNK

    def send(chunk):
        rows = pl.ds(pl.multiple_of(chunk * CHUNK, CHUNK), CHUNK)
        return pltpu.make_async_remote_copy(
            src_ref=out_ref.at[rows],
            dst_ref=gy_ref.at[rows],
            send_sem=send_sem.at[chunk],
            recv_sem=recv_sem.at[chunk],
            device_id=(before, dp),
            device_id_type=MESH,
        )

    def step(chunk, _):
        @pl.when(section < sections - 1)
        def _():
            send(chunk).wait_recv()

        rows = pl.ds(pl.multiple_of(chunk * CHUNK, CHUNK), CHUNK)
        relay_chunk(rows, gy_ref, x_ref, gain_ref, wo_ref, wq_ref, k_ref, vt_ref, p_ref, ga_ref, gs_ref, gq_ref, gn_ref, out_ref)

        @pl.when(section > 0)
        def _():
            send(chunk).start()

        return 0

    lax.fori_loop(0, chunks, step, 0)

    @pl.when(section > 0)
    def _():
        def done(chunk, _):
            send(chunk).wait_send()
            return 0

        lax.fori_loop(0, chunks, done, 0)


def relay(grad_out, x, gain, wo_t, wq_t, keys, values_t, prob):
    rows, width = x.shape
    vmem = pl.BlockSpec(memory_space=pltpu.VMEM)
    return pl.pallas_call(
        relay_kernel,
        out_shape=(
            jax.ShapeDtypeStruct((rows, width), BF16),
            jax.ShapeDtypeStruct((rows, width), BF16),
            jax.ShapeDtypeStruct(prob.shape, BF16),
        ),
        in_specs=[vmem] * 8,
        out_specs=(vmem, vmem, vmem),
        scratch_shapes=[
            pltpu.VMEM((rows, width), BF16),
            pltpu.VMEM((CHUNK, width), BF16),
            pltpu.VMEM((CHUNK, width), F32),
            pltpu.SemaphoreType.DMA((rows // CHUNK,)),
            pltpu.SemaphoreType.DMA((rows // CHUNK,)),
        ],
        compiler_params=pltpu.CompilerParams(
            collective_id=1, has_side_effects=True, vmem_limit_bytes=56 * 2**20
        ),
    )(grad_out, x, gain, wo_t, wq_t, keys, values_t, prob)


def per_device(
    hidden_in, grad_out, encoder_out, enc_valid, norm_gain, w_query, w_key, w_value, w_out
):
    encoded = lax.all_gather(encoder_out, "section", axis=1, tiled=True)[0]
    valid = lax.all_gather(enc_valid.astype(BF16), "section", axis=1, tiled=True)[0].astype(F32)
    own = jnp.stack([w_query[0].T, w_key[0].T, w_out[0].T, w_value[0].T])
    full = gather_weights(own)
    wq_t, wk_t, wo_t, wv_t = full[0], full[1], full[2], full[3]
    x = hidden_in[0, 0]
    x32 = x.astype(F32)
    gain = norm_gain[0].astype(F32)
    inv_rms = lax.rsqrt(jnp.mean(x32 * x32, axis=1, keepdims=True) + 1e-06)
    normed = (x32 * inv_rms * gain).astype(BF16)
    rows, width = x.shape
    blocks = lambda a: a.reshape(rows, 16, 128)
    queries = jnp.einsum("rbd,bid->ri", blocks(normed), wq_t, preferred_element_type=F32).astype(BF16)
    keys = jnp.einsum("rbd,bid->ri", blocks(encoded), wk_t, preferred_element_type=F32).astype(BF16)
    values_t = jnp.einsum("bid,rbd->ir", wv_t, blocks(encoded), preferred_element_type=F32).astype(BF16)
    q_heads = queries.reshape(rows, 32, HEAD)
    k_heads = keys.reshape(rows, 32, HEAD)
    scores = jnp.einsum("lhd,ehd->hle", q_heads, k_heads, preferred_element_type=F32)
    raw = jnp.exp(scores) * valid[None, None, :]
    prob = (raw / jnp.sum(raw, axis=2, keepdims=True)).astype(BF16)
    grad_in, grad_attn, grad_scores = relay(
        grad_out[0], x, norm_gain, wo_t, wq_t, keys, values_t, prob
    )
    ga_heads = grad_attn.reshape(rows, 32, HEAD)
    grad_key = jnp.einsum("hle,lhd->ehd", grad_scores, q_heads, preferred_element_type=F32)
    grad_value = jnp.einsum("hle,lhd->ehd", prob, ga_heads, preferred_element_type=F32)
    grad_key = grad_key.astype(BF16).reshape(rows, width)
    grad_value = grad_value.astype(BF16).reshape(rows, width)
    term = jnp.einsum("ri,bid->rbd", grad_key, wk_t, preferred_element_type=F32)
    term = term + jnp.einsum("ri,bid->rbd", grad_value, wv_t, preferred_element_type=F32)
    enc_grad = lax.psum_scatter(
        term.reshape(rows, width).astype(BF16), "section", scatter_dimension=0, tiled=True
    )
    return (grad_in[None, None], enc_grad[None])


def solution(mesh):
    in_specs = (
        P("section", "dp", None, None),
        P("dp", None, None),
        P("dp", "section", None),
        P("dp", "section"),
        P("section", None),
        P("section", "dp", None),
        P("section", "dp", None),
        P("section", "dp", None),
        P("section", "dp", None),
    )
    out_specs = (P("section", "dp", None, None), P("dp", "section", None))
    return jax.shard_map(
        per_device, mesh=mesh, in_specs=in_specs, out_specs=out_specs, check_vma=False
    )
```

```python
import functools

import jax
import jax.numpy as jnp
from jax import lax
from jax.experimental import pallas as pl
from jax.experimental.pallas import tpu as pltpu
from jax.sharding import PartitionSpec as P

HEAD = 64
MESH = pl.DeviceIdType.MESH
F32 = jnp.float32
BF16 = jnp.bfloat16

FULL = 2048
HALF = FULL // 2
PART_A = 1152
HALF_A = PART_A // 2
COPIES = 27
CHUNK = 32


def copy_plan():
    part_b = FULL - PART_A
    return [
        (0, 0, 0, FULL, "z+"),
        (0, 0, 0, FULL, "z-"),
        (0, 0, 0, PART_A, "y"),
        (0, 0, PART_A, part_b, "y"),
        (0, 0, 0, FULL, "core"),
        (0, -1, 0, HALF, "z+"),
        (0, -1, PART_A, part_b, "y"),
        (0, -1, 0, FULL, "core"),
        (0, 1, HALF, HALF, "z-"),
        (0, 1, PART_A, part_b, "y"),
        (0, 1, 0, FULL, "core"),
        (1, 0, 0, PART_A, "z+"),
        (1, 0, 0, PART_A, "z-"),
        (1, 0, 0, PART_A, "core"),
        (1, 0, PART_A, part_b, "core"),
        (0, 2, 0, HALF, "core"),
        (0, 2, PART_A, part_b, "y"),
        (0, 2, HALF, HALF, "core"),
        (1, -1, 0, HALF_A, "z+"),
        (1, -1, 0, PART_A, "core"),
        (1, 1, HALF_A, HALF_A, "z-"),
        (1, 1, 0, PART_A, "core"),
        (1, -1, PART_A, part_b, "core"),
        (1, 1, PART_A, part_b, "core"),
        (1, 2, 0, HALF_A, "core"),
        (1, 2, HALF_A, HALF_A, "core"),
        (1, 2, PART_A, part_b, "core"),
    ]


PLAN = copy_plan()
STAGES = [
    ((), (0, 1, 2, 3, 4)),
    ((0, 1, 2, 3), (5, 8, 11, 12, 6, 9, 7, 10, 13, 14)),
    ((5, 8, 11, 12, 6, 9), (18, 20, 16, 15, 17, 19, 21, 22, 23)),
    ((18, 20, 16), (24, 25, 26)),
    ((4, 7, 10, 13, 14, 15, 17, 19, 21, 22, 23, 24, 25, 26), ()),
]


class Gather:
    def __init__(self, own_ref, full_ref, send_sem, recv_sem, local_sem):
        self.own, self.full = own_ref, full_ref
        self.send_sem, self.recv_sem, self.local_sem = send_sem, recv_sem, local_sem
        self.section, dp = lax.axis_index("section"), lax.axis_index("dp")
        self.half, self.z, self.core = dp // 8, (dp // 2) % 4, dp % 2

    def dp_of(self, half, z, core):
        return half * 8 + ((z + 4) % 4) * 2 + core

    def target(self, name):
        half, z, core = self.half, self.z, self.core
        dp = {
            "z+": self.dp_of(half, z + 1, core),
            "z-": self.dp_of(half, z + 3, core),
            "y": self.dp_of(1 - half, z, core),
            "core": self.dp_of(half, z, 1 - core),
        }[name]
        return (self.section, dp)

    def greet(self, barrier):
        for name in ("z+", "z-", "y", "core"):
            pl.semaphore_signal(barrier, inc=1, device_id=self.target(name), device_id_type=MESH)
        return 4

    def copy(self, matrix, k):
        half_off, z_off, first, rows, name = PLAN[k]
        half = 1 - self.half if half_off else self.half
        unit = self.dp_of(half, self.z + (z_off + 4) % 4, self.core)
        dst = self.full.at[matrix, unit, pl.ds(first, rows)]
        own = half_off == 0 and z_off == 0
        src = self.own.at[matrix, pl.ds(first, rows)] if own else dst
        return pltpu.make_async_remote_copy(
            src_ref=src,
            dst_ref=dst,
            send_sem=self.send_sem.at[matrix, k],
            recv_sem=self.recv_sem.at[matrix, k],
            device_id=self.target(name),
            device_id_type=MESH,
        )

    def arrival(self, matrix, k):
        return self.copy(matrix, k)

    def local(self, matrix):
        me = self.dp_of(self.half, self.z, self.core)
        return pltpu.make_async_copy(
            self.own.at[matrix], self.full.at[matrix, me], self.local_sem.at[matrix]
        )

    def stage(self, matrix, number):
        waits, starts = STAGES[number]
        if number == 0:
            self.local(matrix).start()
        if number == 1:
            self.local(matrix).wait()
        for k in waits:
            self.arrival(matrix, k).wait_recv()
        for k in starts:
            self.copy(matrix, k).start()

    def finish(self, matrix):
        for k in range(COPIES):
            self.copy(matrix, k).wait_send()


Q, K, O, V = 0, 1, 2, 3
ENC_TILES = 4
NT = (((1,), (1,)), ((), ()))


def wide(ref, blocks, rows=slice(None)):
    return jnp.concatenate([ref[block, rows, :] for block in blocks], axis=1)


def low_lanes(rows):
    return lax.broadcasted_iota(jnp.int32, (rows, 128), 1) < HEAD


def split_heads(pair):
    low = low_lanes(pair.shape[0])
    zero = jnp.zeros(pair.shape, pair.dtype)
    return jnp.concatenate([jnp.where(low, pair, zero), jnp.where(low, zero, pair)], axis=0)


def inverse_rms(x):
    return lax.rsqrt(jnp.sum(x * x, axis=1, keepdims=True) * (1.0 / x.shape[1]) + 1e-06)


def tile_of(index, size):
    return pl.ds(pl.multiple_of(index * size, size), size)


def project(act_ref, weight_ref, out_ref):
    def tile(index, _):
        rows = tile_of(index, 256)
        weight = wide(weight_ref, range(16), rows)
        part = lax.dot_general(act_ref[...], weight, NT, preferred_element_type=F32)
        out_ref[:, rows] = part.astype(BF16)
        return 0

    lax.fori_loop(0, FULL // 256, tile, 0)


def project_values(core, enc_ref, weight_ref, acc_ref, out_ref, last):
    blocks = [2 * i + core for i in range(8)]

    def tile(index, _):
        rows = tile_of(index, 256)
        weight = wide(weight_ref, blocks, rows)
        act = jnp.concatenate([enc_ref[:, tile_of(block, 128)] for block in blocks], axis=1)
        part = lax.dot_general(weight, act, NT, preferred_element_type=F32)
        if last:
            out_ref[rows, :] = (acc_ref[rows, :] + part).astype(BF16)
        else:
            acc_ref[rows, :] = part
        return 0

    lax.fori_loop(0, FULL // 256, tile, 0)


def probabilities(q_ref, k_ref, count_ref, p_ref, qt_ref):
    total = jnp.sum(count_ref[...], axis=0)[0:1, :]
    position = lax.broadcasted_iota(jnp.int32, (1, 256), 1)
    mask = jnp.where(position < jnp.concatenate([total, total], axis=1), 1.0, 0.0)

    def step(pair, _):
        lanes = tile_of(pair, 128)
        query = q_ref[:, lanes]
        scores = lax.dot_general(
            split_heads(query), k_ref[:, lanes], NT, preferred_element_type=F32
        )
        raw = jnp.exp(scores) * mask
        prob = (raw / jnp.sum(raw, axis=1, keepdims=True)).astype(BF16)
        p_ref[2 * pair] = prob[:256]
        p_ref[2 * pair + 1] = prob[256:]
        qt_ref[lanes, :] = query.T
        return 0

    lax.fori_loop(0, 16, step, 0)


def relay_chunk(rows, gy_ref, x_ref, gain_ref, wo_ref, wq_ref, k_ref, vt_ref, p_ref, ga_ref, gs_ref, gq_ref, gn_ref, out_ref):
    grad_y = gy_ref[rows, :]
    for j in range(2):
        part = jnp.dot(grad_y, wide(wo_ref, range(8 * j, 8 * j + 8)), preferred_element_type=F32)
        ga_ref[rows, j * 1024 : (j + 1) * 1024] = part.astype(BF16)
    low = low_lanes(CHUNK)
    for pair in range(16):
        lanes = slice(pair * 128, (pair + 1) * 128)
        both = split_heads(ga_ref[rows, lanes])
        grad_prob = jnp.dot(both, vt_ref[lanes, :], preferred_element_type=F32)
        prob = jnp.concatenate([p_ref[2 * pair, rows, :], p_ref[2 * pair + 1, rows, :]], axis=0)
        prob = prob.astype(F32)
        inner = jnp.sum(prob * grad_prob, axis=1, keepdims=True)
        grad_scores = (prob * (grad_prob - inner)).astype(BF16)
        gs_ref[2 * pair, rows, :] = grad_scores[:CHUNK]
        gs_ref[2 * pair + 1, rows, :] = grad_scores[CHUNK:]
        grad_query = jnp.dot(grad_scores, k_ref[:, lanes], preferred_element_type=F32)
        gq_ref[:, lanes] = jnp.where(low, grad_query[:CHUNK], grad_query[CHUNK:]).astype(BF16)
    grad_query = gq_ref[...]
    for j in range(2):
        gn_ref[:, j * 1024 : (j + 1) * 1024] = jnp.dot(
            grad_query, wide(wq_ref, range(8 * j, 8 * j + 8)), preferred_element_type=F32
        )
    x = x_ref[rows, :].astype(F32)
    inv_rms = inverse_rms(x)
    scaled = gn_ref[...] * gain_ref[...].astype(F32)
    mean = jnp.sum(x * scaled, axis=1, keepdims=True) * (1.0 / x.shape[1])
    branch = inv_rms * scaled - x * (inv_rms * inv_rms * inv_rms * mean)
    out_ref[rows, :] = (grad_y.astype(F32) + branch).astype(BF16)


def key_value_grads(qt_ref, gs_ref, p_ref, ga_ref, gk_ref):
    def step(quad, _):
        for inside in range(4):
            pair = quad * 4 + inside
            lanes = tile_of(pair, 128)
            query_t = qt_ref[lanes, :]
            attn_t = ga_ref[:, lanes].T
            for left, right_ref, out_ref in ((query_t, gs_ref, gk_ref), (attn_t, p_ref, ga_ref)):
                heads = [
                    jnp.dot(
                        left[head * HEAD : (head + 1) * HEAD],
                        right_ref[2 * pair + head],
                        preferred_element_type=F32,
                    )
                    for head in range(2)
                ]
                out_ref[:, lanes] = jnp.concatenate(heads, axis=0).T.astype(BF16)
        return 0

    lax.fori_loop(0, 4, step, 0)


def whole_kernel(
    own_ref, enc_own_ref, count_own_ref, x_ref, gout_ref, gain_ref,
    gin_ref, genc_ref,
    full_ref, enc_ref, count_ref, gy_ref, qt_ref, k_ref, vt_ref, p_ref, gs_ref, ga_ref,
    gq_ref, gn_ref, acc_ref, slot_ref,
    send_sem, recv_sem, local_sem,
    enc_send, enc_recv, count_send, count_recv, relay_send, relay_recv, term_send, term_recv,
):
    sections = lax.axis_size("section")
    section, dp = lax.axis_index("section"), lax.axis_index("dp")
    gather = Gather(own_ref, full_ref, send_sem, recv_sem, local_sem)
    offsets = range(1, sections)

    def other(offset):
        return (section + offset) % sections

    def remote(src, dst, send, recv, to):
        return pltpu.make_async_remote_copy(
            src_ref=src, dst_ref=dst, send_sem=send, recv_sem=recv,
            device_id=(to, dp), device_id_type=MESH,
        )

    barrier = pltpu.get_barrier_semaphore()
    greeted = gather.greet(barrier)
    for offset in offsets:
        pl.semaphore_signal(barrier, inc=1, device_id=(other(offset), dp), device_id_type=MESH)
    pl.semaphore_wait(barrier, greeted + len(offsets))

    my_rows = tile_of(section, enc_own_ref.shape[0])

    def enc_copies(offset):
        return (
            remote(enc_own_ref, enc_ref.at[my_rows], enc_send.at[offset], enc_recv.at[offset], other(offset)),
            remote(count_own_ref, count_ref.at[section], count_send.at[offset], count_recv.at[offset], other(offset)),
        )

    gather.stage(0, 0)
    gather.stage(1, 0)
    for offset in offsets:
        for copy in enc_copies(offset):
            copy.start()
    enc_ref[my_rows, :] = enc_own_ref[...]
    count_ref[section] = count_own_ref[...]

    @pl.when(section == sections - 1)
    def _():
        first = pltpu.make_async_copy(gout_ref, gy_ref, local_sem.at[4])
        first.start()
        first.wait()

    def norm(chunk, _):
        rows = tile_of(chunk, CHUNK)
        x = x_ref[rows, :].astype(F32)
        gin_ref[rows, :] = (x * inverse_rms(x) * gain_ref[...].astype(F32)).astype(BF16)
        return 0

    lax.fori_loop(0, gy_ref.shape[0] // CHUNK, norm, 0)

    for matrix, number in ((0, 1), (2, 0), (1, 1), (0, 2), (3, 0), (2, 1), (1, 2), (0, 3), (0, 4)):
        gather.stage(matrix, number)
    project(gin_ref, full_ref.at[Q], ga_ref)
    for matrix, number in ((3, 1), (2, 2), (1, 3), (1, 4)):
        gather.stage(matrix, number)
    for offset in offsets:
        for copy in enc_copies(offset):
            copy.wait_recv()
    project(enc_ref, full_ref.at[K], k_ref)
    probabilities(ga_ref, k_ref, count_ref, p_ref, qt_ref)
    for matrix, number in ((3, 2), (2, 3), (3, 3)):
        gather.stage(matrix, number)
    project_values(gather.core, enc_ref, full_ref.at[V], acc_ref, vt_ref, False)
    for matrix, number in ((2, 4), (3, 4)):
        gather.stage(matrix, number)
    project_values(1 - gather.core, enc_ref, full_ref.at[V], acc_ref, vt_ref, True)

    chunks = gy_ref.shape[0] // CHUNK

    def send(chunk):
        rows = tile_of(chunk, CHUNK)
        return remote(
            gin_ref.at[rows], gy_ref.at[rows], relay_send.at[chunk], relay_recv.at[chunk], other(sections - 1)
        )

    def step(chunk, _):
        @pl.when(section < sections - 1)
        def _():
            send(chunk).wait_recv()

        relay_chunk(
            tile_of(chunk, CHUNK), gy_ref, x_ref, gain_ref, full_ref.at[O], full_ref.at[Q],
            k_ref, vt_ref, p_ref, ga_ref, gs_ref, gq_ref, gn_ref, gin_ref,
        )

        @pl.when(section > 0)
        def _():
            send(chunk).start()

        return 0

    lax.fori_loop(0, chunks, step, 0)

    key_value_grads(qt_ref, gs_ref, p_ref, ga_ref, k_ref)
    width = FULL // ENC_TILES
    enc_rows = enc_own_ref.shape[0]

    def term_copy(tile, offset):
        cols = pl.ds(tile * width, width)
        return remote(
            enc_ref.at[tile_of(other(offset), enc_rows), cols], slot_ref.at[offset, :, cols],
            term_send.at[tile, offset], term_recv.at[tile, offset], other(offset),
        )

    for tile in range(ENC_TILES):
        blocks = range(tile * 16 // ENC_TILES, (tile + 1) * 16 // ENC_TILES)
        part = jnp.dot(k_ref[...], wide(full_ref.at[K], blocks), preferred_element_type=F32)
        part = part + jnp.dot(ga_ref[...], wide(full_ref.at[V], blocks), preferred_element_type=F32)
        enc_ref[:, tile * width : (tile + 1) * width] = part.astype(BF16)
        for offset in offsets:
            term_copy(tile, offset).start()
    for tile in range(ENC_TILES):
        for offset in offsets:
            term_copy(tile, offset).wait_recv()
    total = enc_ref[my_rows, :].astype(F32)
    for offset in offsets:
        total = total + slot_ref[offset].astype(F32)
    genc_ref[...] = total.astype(BF16)

    for matrix in range(4):
        gather.finish(matrix)
    for offset in offsets:
        for copy in enc_copies(offset):
            copy.wait_send()
        for tile in range(ENC_TILES):
            term_copy(tile, offset).wait_send()

    @pl.when(section > 0)
    def _():
        def done(chunk, _):
            send(chunk).wait_send()
            return 0

        lax.fori_loop(0, chunks, done, 0)


def whole(own, enc_own, count_own, x, grad_out, gain):
    rows, width = x.shape
    sections = lax.axis_size("section")
    enc_rows = enc_own.shape[0]
    vmem = pl.BlockSpec(memory_space=pltpu.VMEM)
    any_space = pl.BlockSpec(memory_space=pl.ANY)
    dma = pltpu.SemaphoreType.DMA
    half = pltpu.VMEM((rows, width), BF16)
    turned = pltpu.VMEM((width, rows), BF16)
    per_head = pltpu.VMEM((width // HEAD, rows, rows), BF16)
    return pl.pallas_call(
        whole_kernel,
        out_shape=(
            jax.ShapeDtypeStruct((rows, width), BF16),
            jax.ShapeDtypeStruct((enc_rows, width), BF16),
        ),
        in_specs=[any_space, vmem, vmem, vmem, any_space, vmem],
        out_specs=(vmem, vmem),
        scratch_shapes=[
            pltpu.VMEM((4, 16, FULL, 128), BF16),
            half,
            pltpu.VMEM((sections, 8, 128), jnp.int32),
            half,
            turned,
            half,
            turned,
            per_head,
            per_head,
            half,
            pltpu.VMEM((CHUNK, width), BF16),
            pltpu.VMEM((CHUNK, width), F32),
            pltpu.VMEM((width, rows), F32),
            pltpu.VMEM((sections, enc_rows, width), BF16),
            dma((4, COPIES)),
            dma((4, COPIES)),
            dma((5,)),
            dma((sections,)),
            dma((sections,)),
            dma((sections,)),
            dma((sections,)),
            dma((rows // CHUNK,)),
            dma((rows // CHUNK,)),
            dma((ENC_TILES, sections)),
            dma((ENC_TILES, sections)),
        ],
        compiler_params=pltpu.CompilerParams(
            collective_id=0, has_side_effects=True, vmem_limit_bytes=60 * 2**20
        ),
    )(own, enc_own, count_own, x, grad_out, gain)


def per_device(
    hidden_in, grad_out, encoder_out, enc_valid, norm_gain, w_query, w_key, w_value, w_out
):
    own = jnp.stack([w_query[0].T, w_key[0].T, w_out[0].T, w_value[0].T])
    count = jnp.broadcast_to(jnp.sum(enc_valid), (8, 128))
    grad_in, enc_grad = whole(own, encoder_out[0], count, hidden_in[0, 0], grad_out[0], norm_gain)
    return (grad_in[None, None], enc_grad[None])


def solution(mesh):
    in_specs = (
        P("section", "dp", None, None),
        P("dp", None, None),
        P("dp", "section", None),
        P("dp", "section"),
        P("section", None),
        P("section", "dp", None),
        P("section", "dp", None),
        P("section", "dp", None),
        P("section", "dp", None),
    )
    out_specs = (P("section", "dp", None, None), P("dp", "section", None))
    return jax.shard_map(
        per_device, mesh=mesh, in_specs=in_specs, out_specs=out_specs, check_vma=False
    )
```

```python
import functools

import jax
import jax.numpy as jnp
from jax import lax
from jax.experimental import pallas as pl
from jax.experimental.pallas import tpu as pltpu
from jax.sharding import PartitionSpec as P

HEAD = 64
MESH = pl.DeviceIdType.MESH
F32 = jnp.float32
BF16 = jnp.bfloat16

FULL = 2048
HALF = FULL // 2
PART_A = 1152
HALF_A = PART_A // 2
COPIES = 27
CHUNK = 32
TILES = 4
TILE = 2048 // TILES


def copy_plan():
    part_b = FULL - PART_A
    return [
        (0, 0, 0, FULL, "z+"),
        (0, 0, 0, FULL, "z-"),
        (0, 0, 0, PART_A, "y"),
        (0, 0, PART_A, part_b, "y"),
        (0, 0, 0, FULL, "core"),
        (0, -1, 0, HALF, "z+"),
        (0, -1, PART_A, part_b, "y"),
        (0, -1, 0, FULL, "core"),
        (0, 1, HALF, HALF, "z-"),
        (0, 1, PART_A, part_b, "y"),
        (0, 1, 0, FULL, "core"),
        (1, 0, 0, PART_A, "z+"),
        (1, 0, 0, PART_A, "z-"),
        (1, 0, 0, PART_A, "core"),
        (1, 0, PART_A, part_b, "core"),
        (0, 2, 0, HALF, "core"),
        (0, 2, PART_A, part_b, "y"),
        (0, 2, HALF, HALF, "core"),
        (1, -1, 0, HALF_A, "z+"),
        (1, -1, 0, PART_A, "core"),
        (1, 1, HALF_A, HALF_A, "z-"),
        (1, 1, 0, PART_A, "core"),
        (1, -1, PART_A, part_b, "core"),
        (1, 1, PART_A, part_b, "core"),
        (1, 2, 0, HALF_A, "core"),
        (1, 2, HALF_A, HALF_A, "core"),
        (1, 2, PART_A, part_b, "core"),
    ]


PLAN = copy_plan()
STAGES = [
    ((), (0, 1, 2, 3, 4)),
    ((0, 1, 2, 3), (5, 8, 11, 12, 6, 9, 7, 10, 13, 14)),
    ((5, 8, 11, 12, 6, 9), (18, 20, 16, 15, 17, 19, 21, 22, 23)),
    ((18, 20, 16), (24, 25, 26)),
    ((4, 7, 10, 13, 14, 15, 17, 19, 21, 22, 23, 24, 25, 26), ()),
]


class Gather:
    def __init__(self, shard_refs, full_ref, send_sem, recv_sem):
        self.shards, self.full = shard_refs, full_ref
        self.send_sem, self.recv_sem = send_sem, recv_sem
        self.section, dp = lax.axis_index("section"), lax.axis_index("dp")
        self.half, self.z, self.core = dp // 8, (dp // 2) % 4, dp % 2

    def dp_of(self, half, z, core):
        return half * 8 + ((z + 4) % 4) * 2 + core

    def target(self, name):
        half, z, core = self.half, self.z, self.core
        dp = {
            "z+": self.dp_of(half, z + 1, core),
            "z-": self.dp_of(half, z + 3, core),
            "y": self.dp_of(1 - half, z, core),
            "core": self.dp_of(half, z, 1 - core),
        }[name]
        return (self.section, dp)

    def greet(self, barrier):
        for name in ("z+", "z-", "y", "core"):
            pl.semaphore_signal(barrier, inc=1, device_id=self.target(name), device_id_type=MESH)
        return 4

    def turn(self, matrix):
        me = self.dp_of(self.half, self.z, self.core)
        shard = self.shards[matrix]

        def step(quad, _):
            for inside in range(4):
                lanes = tile_of(quad * 4 + inside, 128)
                self.full[matrix, me, lanes, :] = shard[:, lanes].T
            return 0

        lax.fori_loop(0, FULL // 512, step, 0)

    def copy(self, matrix, k):
        half_off, z_off, first, rows, name = PLAN[k]
        half = 1 - self.half if half_off else self.half
        unit = self.dp_of(half, self.z + (z_off + 4) % 4, self.core)
        block = self.full.at[matrix, unit, pl.ds(first, rows)]
        return pltpu.make_async_remote_copy(
            src_ref=block,
            dst_ref=block,
            send_sem=self.send_sem.at[matrix, k],
            recv_sem=self.recv_sem.at[matrix, k],
            device_id=self.target(name),
            device_id_type=MESH,
        )

    def stage(self, matrix, number):
        waits, starts = STAGES[number]
        for k in waits:
            self.copy(matrix, k).wait_recv()
        for k in starts:
            self.copy(matrix, k).start()

    def finish(self, matrix):
        for k in range(COPIES):
            self.copy(matrix, k).wait_send()


Q, K, O, V = 0, 1, 2, 3
ENC_TILES = 4
NT = (((1,), (1,)), ((), ()))


def wide(ref, blocks, rows=slice(None)):
    return jnp.concatenate([ref[block, rows, :] for block in blocks], axis=1)


def low_lanes(rows):
    return lax.broadcasted_iota(jnp.int32, (rows, 128), 1) < HEAD


def split_heads(pair):
    low = low_lanes(pair.shape[0])
    zero = jnp.zeros(pair.shape, pair.dtype)
    return jnp.concatenate([jnp.where(low, pair, zero), jnp.where(low, zero, pair)], axis=0)


def inverse_rms(x):
    return lax.rsqrt(jnp.sum(x * x, axis=1, keepdims=True) * (1.0 / x.shape[1]) + 1e-06)


def tile_of(index, size):
    return pl.ds(pl.multiple_of(index * size, size), size)


def project(act_ref, weight_ref, out_ref):
    def tile(index, _):
        rows = tile_of(index, 256)
        weight = wide(weight_ref, range(16), rows)
        part = lax.dot_general(act_ref[...], weight, NT, preferred_element_type=F32)
        out_ref[:, rows] = part.astype(BF16)
        return 0

    lax.fori_loop(0, FULL // 256, tile, 0)


def project_values(core, enc_ref, weight_ref, acc_ref, out_ref, last):
    blocks = [2 * i + core for i in range(8)]

    def tile(index, _):
        rows = tile_of(index, 256)
        weight = wide(weight_ref, blocks, rows)
        act = jnp.concatenate([enc_ref[:, tile_of(block, 128)] for block in blocks], axis=1)
        part = lax.dot_general(weight, act, NT, preferred_element_type=F32)
        if last:
            out_ref[rows, :] = (acc_ref[rows, :] + part).astype(BF16)
        else:
            acc_ref[rows, :] = part
        return 0

    lax.fori_loop(0, FULL // 256, tile, 0)


def probabilities(q_ref, k_ref, count_ref, p_ref, qt_ref):
    total = jnp.sum(count_ref[...], axis=0)[0:1, :]
    position = lax.broadcasted_iota(jnp.int32, (1, 256), 1).astype(F32)
    mask = jnp.where(position < jnp.concatenate([total, total], axis=1), 1.0, 0.0)

    def step(pair, _):
        lanes = tile_of(pair, 128)
        query = q_ref[:, lanes]
        scores = lax.dot_general(
            split_heads(query), k_ref[:, lanes], NT, preferred_element_type=F32
        )
        raw = jnp.exp(scores) * mask
        prob = (raw / jnp.sum(raw, axis=1, keepdims=True)).astype(BF16)
        p_ref[2 * pair] = prob[:256]
        p_ref[2 * pair + 1] = prob[256:]
        qt_ref[lanes, :] = query.T
        return 0

    lax.fori_loop(0, 16, step, 0)


def relay_attention(rows, arrive, gy_ref, wo_ref, q_ref, k_ref, vt_ref, p_ref, ga_ref, gs_ref, gq_ref, sum_ref, dot_ref):
    for tile in range(TILES):
        arrive(tile)
        cols = slice(tile * TILE, (tile + 1) * TILE)
        grad_y = gy_ref[rows, cols]
        for j in range(2):
            lanes = slice(j * 1024, (j + 1) * 1024)
            weight = wide(wo_ref, range(8 * j, 8 * j + 8), cols)
            part = jnp.dot(grad_y, weight, preferred_element_type=F32)
            if tile:
                part = sum_ref[:, lanes] + part
            if tile < TILES - 1:
                sum_ref[:, lanes] = part
            else:
                ga_ref[rows, lanes] = part.astype(BF16)
    low = low_lanes(CHUNK)
    product = jnp.zeros((CHUNK, 128), F32)
    for pair in range(16):
        lanes = slice(pair * 128, (pair + 1) * 128)
        both = split_heads(ga_ref[rows, lanes])
        grad_prob = jnp.dot(both, vt_ref[lanes, :], preferred_element_type=F32)
        prob = jnp.concatenate([p_ref[2 * pair, rows, :], p_ref[2 * pair + 1, rows, :]], axis=0)
        prob = prob.astype(F32)
        inner = jnp.sum(prob * grad_prob, axis=1, keepdims=True)
        grad_scores = (prob * (grad_prob - inner)).astype(BF16)
        gs_ref[2 * pair, rows, :] = grad_scores[:CHUNK]
        gs_ref[2 * pair + 1, rows, :] = grad_scores[CHUNK:]
        both_query = jnp.dot(grad_scores, k_ref[:, lanes], preferred_element_type=F32)
        grad_query = jnp.where(low, both_query[:CHUNK], both_query[CHUNK:]).astype(BF16)
        gq_ref[:, lanes] = grad_query
        product = product + grad_query.astype(F32) * q_ref[rows, lanes].astype(F32)
    dot_ref[...] = jnp.sum(product, axis=1, keepdims=True) + jnp.zeros((CHUNK, 128), F32)


def relay_output(rows, leave, gy_ref, x_ref, gain_ref, inv_ref, wq_ref, gq_ref, dot_ref, out_ref):
    inv_rms = inv_ref[rows, 0:1]
    x_scale = inv_rms * inv_rms * dot_ref[:, 0:1] * (1.0 / FULL)
    grad_query = gq_ref[...]
    for tile in range(TILES):
        cols = slice(tile * TILE, (tile + 1) * TILE)
        blocks = range(tile * 16 // TILES, (tile + 1) * 16 // TILES)
        grad_normed = jnp.dot(grad_query, wide(wq_ref, blocks), preferred_element_type=F32)
        scaled = grad_normed * gain_ref[:, cols].astype(F32)
        branch = inv_rms * scaled - x_ref[rows, cols].astype(F32) * x_scale
        out_ref[rows, cols] = (gy_ref[rows, cols].astype(F32) + branch).astype(BF16)
        leave(tile)


def key_value_grads(qt_ref, gs_ref, p_ref, ga_ref, gk_ref):
    def step(quad, _):
        for inside in range(4):
            pair = quad * 4 + inside
            lanes = tile_of(pair, 128)
            query_t = qt_ref[lanes, :]
            attn_t = ga_ref[:, lanes].T
            for left, right_ref, out_ref in ((query_t, gs_ref, gk_ref), (attn_t, p_ref, ga_ref)):
                heads = [
                    jnp.dot(
                        left[head * HEAD : (head + 1) * HEAD],
                        right_ref[2 * pair + head],
                        preferred_element_type=F32,
                    )
                    for head in range(2)
                ]
                out_ref[:, lanes] = jnp.concatenate(heads, axis=0).T.astype(BF16)
        return 0

    lax.fori_loop(0, 4, step, 0)


def whole_kernel(
    wq_own_ref, wk_own_ref, wo_own_ref, wv_own_ref, enc_own_ref, valid_ref, x_ref, gout_ref, gain_ref,
    gin_ref, genc_ref,
    full_ref, enc_ref, count_own_ref, count_ref, gy_ref, q_ref, qt_ref, k_ref, vt_ref, p_ref, gs_ref, ga_ref,
    gq_ref, sum_ref, dot_ref, inv_ref, acc_ref, slot_ref,
    send_sem, recv_sem, local_sem,
    enc_send, enc_recv, count_send, count_recv, relay_send, relay_recv, term_send, term_recv,
):
    sections = lax.axis_size("section")
    section, dp = lax.axis_index("section"), lax.axis_index("dp")
    gather = Gather((wq_own_ref, wk_own_ref, wo_own_ref, wv_own_ref), full_ref, send_sem, recv_sem)
    offsets = range(1, sections)

    def other(offset):
        return (section + offset) % sections

    def remote(src, dst, send, recv, to):
        return pltpu.make_async_remote_copy(
            src_ref=src, dst_ref=dst, send_sem=send, recv_sem=recv,
            device_id=(to, dp), device_id_type=MESH,
        )

    barrier = pltpu.get_barrier_semaphore()
    greeted = gather.greet(barrier)
    for offset in offsets:
        pl.semaphore_signal(barrier, inc=1, device_id=(other(offset), dp), device_id_type=MESH)
    gather.turn(0)
    valid = jnp.sum(valid_ref[...].astype(F32), axis=1, keepdims=True)
    count_own_ref[...] = jnp.broadcast_to(valid, count_own_ref.shape)
    pl.semaphore_wait(barrier, greeted + len(offsets))

    my_rows = tile_of(section, enc_own_ref.shape[0])

    def enc_copies(offset):
        return (
            remote(enc_own_ref, enc_ref.at[my_rows], enc_send.at[offset], enc_recv.at[offset], other(offset)),
            remote(count_own_ref, count_ref.at[section], count_send.at[offset], count_recv.at[offset], other(offset)),
        )

    gather.stage(0, 0)
    gather.turn(1)
    gather.stage(1, 0)
    for offset in offsets:
        for copy in enc_copies(offset):
            copy.start()
    enc_ref[my_rows, :] = enc_own_ref[...]
    count_ref[section] = count_own_ref[...]
    gather.turn(2)
    gather.turn(3)

    @pl.when(section == sections - 1)
    def _():
        pltpu.make_async_copy(gout_ref, gy_ref, local_sem.at[0]).start()

    def norm(chunk, _):
        rows = tile_of(chunk, 32)
        x = x_ref[rows, :].astype(F32)
        inv_rms = inverse_rms(x)
        inv_ref[rows, :] = jnp.broadcast_to(inv_rms, (32, 128))
        gin_ref[rows, :] = (x * inv_rms * gain_ref[...].astype(F32)).astype(BF16)
        return 0

    lax.fori_loop(0, gy_ref.shape[0] // 32, norm, 0)

    for matrix, number in ((0, 1), (2, 0), (1, 1), (0, 2), (3, 0), (2, 1), (1, 2), (0, 3), (0, 4)):
        gather.stage(matrix, number)
    project(gin_ref, full_ref.at[Q], q_ref)
    for matrix, number in ((3, 1), (2, 2), (1, 3), (1, 4)):
        gather.stage(matrix, number)
    for offset in offsets:
        for copy in enc_copies(offset):
            copy.wait_recv()
    project(enc_ref, full_ref.at[K], k_ref)
    probabilities(q_ref, k_ref, count_ref, p_ref, qt_ref)
    for matrix, number in ((3, 2), (2, 3), (3, 3)):
        gather.stage(matrix, number)
    project_values(gather.core, enc_ref, full_ref.at[V], acc_ref, vt_ref, False)
    for matrix, number in ((2, 4), (3, 4)):
        gather.stage(matrix, number)
    project_values(1 - gather.core, enc_ref, full_ref.at[V], acc_ref, vt_ref, True)

    @pl.when(section == sections - 1)
    def _():
        pltpu.make_async_copy(gout_ref, gy_ref, local_sem.at[0]).wait()

    chunks = gy_ref.shape[0] // CHUNK

    def send(chunk, tile):
        rows, cols = tile_of(chunk, CHUNK), pl.ds(tile * TILE, TILE)
        return remote(
            gin_ref.at[rows, cols], gy_ref.at[rows, cols],
            relay_send.at[chunk, tile], relay_recv.at[chunk, tile], other(sections - 1),
        )

    def attention(chunk):
        def arrive(tile):
            @pl.when(section < sections - 1)
            def _():
                send(chunk, tile).wait_recv()

        relay_attention(
            tile_of(chunk, CHUNK), arrive, gy_ref, full_ref.at[O], q_ref, k_ref, vt_ref, p_ref,
            ga_ref, gs_ref, gq_ref, sum_ref, dot_ref,
        )

    def output(chunk, leave):
        relay_output(
            tile_of(chunk, CHUNK), leave, gy_ref, x_ref, gain_ref, inv_ref, full_ref.at[Q],
            gq_ref, dot_ref, gin_ref,
        )

    def step(chunk, _):
        attention(chunk)

        @pl.when(jnp.logical_or(section > 0, chunk < chunks - 1))
        def _():
            def leave(tile):
                @pl.when(section > 0)
                def _():
                    send(chunk, tile).start()

            output(chunk, leave)

        return 0

    lax.fori_loop(0, chunks, step, 0)

    key_value_grads(qt_ref, gs_ref, p_ref, ga_ref, k_ref)
    width = FULL // ENC_TILES
    enc_rows = enc_own_ref.shape[0]

    def term_copy(tile, offset):
        cols = pl.ds(tile * width, width)
        return remote(
            enc_ref.at[tile_of(other(offset), enc_rows), cols], slot_ref.at[offset, :, cols],
            term_send.at[tile, offset], term_recv.at[tile, offset], other(offset),
        )

    for tile in range(ENC_TILES):
        blocks = range(tile * 16 // ENC_TILES, (tile + 1) * 16 // ENC_TILES)
        part = jnp.dot(k_ref[...], wide(full_ref.at[K], blocks), preferred_element_type=F32)
        part = part + jnp.dot(ga_ref[...], wide(full_ref.at[V], blocks), preferred_element_type=F32)
        enc_ref[:, tile * width : (tile + 1) * width] = part.astype(BF16)
        for offset in offsets:
            term_copy(tile, offset).start()

    @pl.when(section == 0)
    def _():
        output(chunks - 1, lambda tile: None)

    for matrix in range(4):
        gather.finish(matrix)
    for offset in offsets:
        for copy in enc_copies(offset):
            copy.wait_send()

    @pl.when(section > 0)
    def _():
        def done(chunk, _):
            for tile in range(TILES):
                send(chunk, tile).wait_send()
            return 0

        lax.fori_loop(0, chunks, done, 0)

    for tile in range(ENC_TILES):
        cols = slice(tile * width, (tile + 1) * width)
        total = enc_ref[my_rows, cols].astype(F32)
        for offset in offsets:
            term_copy(tile, offset).wait_recv()
            total = total + slot_ref[offset, :, cols].astype(F32)
        genc_ref[:, cols] = total.astype(BF16)
    for tile in range(ENC_TILES):
        for offset in offsets:
            term_copy(tile, offset).wait_send()


def whole(shards, enc_own, valid, x, grad_out, gain):
    rows, width = x.shape
    sections = lax.axis_size("section")
    enc_rows = enc_own.shape[0]
    chunks = rows // CHUNK
    vmem = pl.BlockSpec(memory_space=pltpu.VMEM)
    any_space = pl.BlockSpec(memory_space=pl.ANY)
    dma = pltpu.SemaphoreType.DMA
    half = pltpu.VMEM((rows, width), BF16)
    turned = pltpu.VMEM((width, rows), BF16)
    per_head = pltpu.VMEM((width // HEAD, rows, rows), BF16)
    return pl.pallas_call(
        whole_kernel,
        out_shape=(
            jax.ShapeDtypeStruct((rows, width), BF16),
            jax.ShapeDtypeStruct((enc_rows, width), BF16),
        ),
        in_specs=[vmem] * 7 + [any_space, vmem],
        out_specs=(vmem, vmem),
        scratch_shapes=[
            pltpu.VMEM((4, 16, FULL, 128), BF16),
            half,
            pltpu.VMEM((8, 128), F32),
            pltpu.VMEM((sections, 8, 128), F32),
            half,
            half,
            turned,
            half,
            turned,
            per_head,
            per_head,
            half,
            pltpu.VMEM((CHUNK, width), BF16),
            pltpu.VMEM((CHUNK, width), F32),
            pltpu.VMEM((CHUNK, 128), F32),
            pltpu.VMEM((rows, 128), F32),
            pltpu.VMEM((width, rows), F32),
            pltpu.VMEM((sections, enc_rows, width), BF16),
            dma((4, COPIES)),
            dma((4, COPIES)),
            dma((1,)),
            dma((sections,)),
            dma((sections,)),
            dma((sections,)),
            dma((sections,)),
            dma((chunks, TILES)),
            dma((chunks, TILES)),
            dma((ENC_TILES, sections)),
            dma((ENC_TILES, sections)),
        ],
        compiler_params=pltpu.CompilerParams(
            collective_id=0, has_side_effects=True, vmem_limit_bytes=60 * 2**20
        ),
    )(*shards, enc_own, valid, x, grad_out, gain)


def per_device(
    hidden_in, grad_out, encoder_out, enc_valid, norm_gain, w_query, w_key, w_value, w_out
):
    shards = (w_query[0], w_key[0], w_out[0], w_value[0])
    grad_in, enc_grad = whole(
        shards, encoder_out[0], enc_valid, hidden_in[0, 0], grad_out[0], norm_gain
    )
    return (grad_in[None, None], enc_grad[None])


def solution(mesh):
    in_specs = (
        P("section", "dp", None, None),
        P("dp", None, None),
        P("dp", "section", None),
        P("dp", "section"),
        P("section", None),
        P("section", "dp", None),
        P("section", "dp", None),
        P("section", "dp", None),
        P("section", "dp", None),
    )
    out_specs = (P("section", "dp", None, None), P("dp", "section", None))
    return jax.shard_map(
        per_device, mesh=mesh, in_specs=in_specs, out_specs=out_specs, check_vma=False
    )
```

```python
import functools

import jax
import jax.numpy as jnp
from jax import lax
from jax.experimental import pallas as pl
from jax.experimental.pallas import tpu as pltpu
from jax.sharding import PartitionSpec as P

HEAD = 64
MESH = pl.DeviceIdType.MESH
F32 = jnp.float32
BF16 = jnp.bfloat16

FULL = 2048
HALF = FULL // 2
PART_A = 1280
HALF_A = PART_A // 2
COPIES = 31
DETOUR = 704
CHUNK = 32
TILES = 4
TILE = 2048 // TILES


def copy_plan():
    part_b = FULL - PART_A
    return [
        (0, 0, 0, HALF, "z+"),
        (0, 0, DETOUR, FULL - DETOUR, "z-"),
        (0, 0, 0, PART_A, "y"),
        (0, 0, PART_A + DETOUR, part_b - DETOUR, "y"),
        (0, 0, 0, FULL, "core"),
        (0, -1, 0, HALF, "z+"),
        (0, -1, PART_A, part_b, "y"),
        (0, -1, 0, FULL, "core"),
        (0, 1, HALF, HALF, "z-"),
        (0, 1, PART_A, part_b, "y"),
        (0, 1, 0, FULL, "core"),
        (1, 0, 0, PART_A, "z+"),
        (1, 0, 0, PART_A, "z-"),
        (1, 0, 0, PART_A, "core"),
        (1, 0, PART_A, part_b, "core"),
        (0, 2, 0, HALF, "core"),
        (0, 2, PART_A, part_b, "y"),
        (0, 2, HALF, HALF, "core"),
        (1, -1, 0, HALF_A, "z+"),
        (1, -1, 0, PART_A, "core"),
        (1, 1, HALF_A, HALF_A, "z-"),
        (1, 1, 0, PART_A, "core"),
        (1, -1, PART_A, part_b, "core"),
        (1, 1, PART_A, part_b, "core"),
        (1, 2, 0, HALF_A, "core"),
        (1, 2, HALF_A, HALF_A, "core"),
        (1, 2, PART_A, part_b, "core"),
        (0, 0, HALF, DETOUR, "z+"),
        (0, 0, 0, DETOUR, "z-"),
        (0, 0, PART_A, DETOUR, "y"),
        (0, 0, HALF + DETOUR, HALF - DETOUR, "z+"),
    ]


PLAN = copy_plan()
DETOURS = (27, 28, 29)
STAGES = [
    ((), (27, 28, 29, 0, 1, 2, 3, 30, 4)),
    ((0, 1, 2, 3, 30), (5, 8, 11, 12, 9, 13)),
    ((27, 28, 29), (6, 7, 10, 14)),
    ((5, 8, 11, 12, 9), (18, 20, 16, 15, 17, 19, 21, 23)),
    ((18, 20, 16, 6), (24, 25, 26, 22)),
    ((4, 7, 10, 13, 14, 15, 17, 19, 21, 22, 23, 24, 25, 26), ()),
]


class Gather:
    def __init__(self, shard_refs, full_ref, send_sem, recv_sem, transit_ref, transit_send, transit_recv):
        self.shards, self.full = shard_refs, full_ref
        self.transit_ref, self.transit_send, self.transit_recv = transit_ref, transit_send, transit_recv
        self.send_sem, self.recv_sem = send_sem, recv_sem
        self.section, dp = lax.axis_index("section"), lax.axis_index("dp")
        self.half, self.z, self.core = dp // 8, (dp // 2) % 4, dp % 2

    def dp_of(self, half, z, core):
        return half * 8 + ((z + 4) % 4) * 2 + core

    def target(self, name):
        half, z, core = self.half, self.z, self.core
        dp = {
            "z+": self.dp_of(half, z + 1, core),
            "z-": self.dp_of(half, z + 3, core),
            "y": self.dp_of(1 - half, z, core),
            "core": self.dp_of(half, z, 1 - core),
        }[name]
        return (self.section, dp)

    def greet(self, barrier):
        for name in ("z+", "z-", "y", "core"):
            pl.semaphore_signal(barrier, inc=1, device_id=self.target(name), device_id_type=MESH)
        self.away = lax.axis_size("section") - 2

        @pl.when(self.section < 2)
        def _():
            for name in ("z+", "z-", "y"):
                _, dp = self.target(name)
                pl.semaphore_signal(
                    barrier, inc=1, device_id=(self.section + self.away, dp), device_id_type=MESH
                )

        return 4

    def detour(self, matrix, index):
        k = DETOURS[index]
        _, dp = self.target(PLAN[k][4])
        me = self.dp_of(self.half, self.z, self.core)
        return pltpu.make_async_remote_copy(
            src_ref=self.full.at[matrix, me, pl.ds(PLAN[k][2], DETOUR)],
            dst_ref=self.transit_ref.at[matrix, index],
            send_sem=self.send_sem.at[matrix, k],
            recv_sem=self.transit_recv.at[matrix, index],
            device_id=(self.section - self.away, dp),
            device_id_type=MESH,
        )

    def onward(self, matrix, index):
        half, z, core = self.half, self.z, self.core
        unit = (self.dp_of(half, z + 3, core), self.dp_of(half, z + 1, core), self.dp_of(1 - half, z, core))[index]
        return pltpu.make_async_remote_copy(
            src_ref=self.transit_ref.at[matrix, index],
            dst_ref=self.full.at[matrix, unit, pl.ds(PLAN[DETOURS[index]][2], DETOUR)],
            send_sem=self.transit_send.at[matrix, index],
            recv_sem=self.recv_sem.at[matrix, DETOURS[index]],
            device_id=(self.section + self.away, self.dp_of(half, z, core)),
            device_id_type=MESH,
        )

    def help(self, matrix):
        @pl.when(self.section < 2)
        def _():
            for index in range(3):
                self.detour(matrix, index).wait_recv()
                self.onward(matrix, index).start()

    def turn(self, matrix):
        me = self.dp_of(self.half, self.z, self.core)
        shard = self.shards[matrix]

        def step(quad, _):
            for inside in range(4):
                lanes = tile_of(quad * 4 + inside, 128)
                self.full[matrix, me, lanes, :] = shard[:, lanes].T
            return 0

        lax.fori_loop(0, FULL // 512, step, 0)

    def copy(self, matrix, k):
        half_off, z_off, first, rows, name = PLAN[k]
        half = 1 - self.half if half_off else self.half
        unit = self.dp_of(half, self.z + (z_off + 4) % 4, self.core)
        block = self.full.at[matrix, unit, pl.ds(first, rows)]
        return pltpu.make_async_remote_copy(
            src_ref=block,
            dst_ref=block,
            send_sem=self.send_sem.at[matrix, k],
            recv_sem=self.recv_sem.at[matrix, k],
            device_id=self.target(name),
            device_id_type=MESH,
        )

    def stage(self, matrix, number):
        waits, starts = STAGES[number]
        for k in waits:
            self.copy(matrix, k).wait_recv()
        for k in starts:
            if k in DETOURS:
                @pl.when(self.section >= self.away)
                def _():
                    self.detour(matrix, DETOURS.index(k)).start()

                @pl.when(self.section < self.away)
                def _():
                    self.copy(matrix, k).start()
            else:
                self.copy(matrix, k).start()

    def finish(self, matrix):
        for k in range(COPIES):
            self.copy(matrix, k).wait_send()

        @pl.when(self.section < 2)
        def _():
            for index in range(3):
                self.onward(matrix, index).wait_send()


Q, K, O, V = 0, 1, 2, 3
ENC_TILES = 4
NT = (((1,), (1,)), ((), ()))


def wide(ref, blocks, rows=slice(None)):
    return jnp.concatenate([ref[block, rows, :] for block in blocks], axis=1)


def low_lanes(rows):
    return lax.broadcasted_iota(jnp.int32, (rows, 128), 1) < HEAD


def split_heads(pair):
    low = low_lanes(pair.shape[0])
    zero = jnp.zeros(pair.shape, pair.dtype)
    return jnp.concatenate([jnp.where(low, pair, zero), jnp.where(low, zero, pair)], axis=0)


def inverse_rms(x):
    return lax.rsqrt(jnp.sum(x * x, axis=1, keepdims=True) * (1.0 / x.shape[1]) + 1e-06)


def tile_of(index, size):
    return pl.ds(pl.multiple_of(index * size, size), size)


def project(act_ref, weight_ref, out_ref):
    def tile(index, _):
        rows = tile_of(index, 256)
        weight = wide(weight_ref, range(16), rows)
        part = lax.dot_general(act_ref[...], weight, NT, preferred_element_type=F32)
        out_ref[:, rows] = part.astype(BF16)
        return 0

    lax.fori_loop(0, FULL // 256, tile, 0)


def project_values(core, enc_ref, weight_ref, acc_ref, out_ref, last):
    blocks = [2 * i + core for i in range(8)]

    def tile(index, _):
        rows = tile_of(index, 256)
        weight = wide(weight_ref, blocks, rows)
        act = jnp.concatenate([enc_ref[:, tile_of(block, 128)] for block in blocks], axis=1)
        part = lax.dot_general(weight, act, NT, preferred_element_type=F32)
        if last:
            out_ref[rows, :] = (acc_ref[rows, :] + part).astype(BF16)
        else:
            acc_ref[rows, :] = part
        return 0

    lax.fori_loop(0, FULL // 256, tile, 0)


def probabilities(q_ref, k_ref, count_ref, p_ref, qt_ref):
    total = jnp.sum(count_ref[...], axis=0)[0:1, :]
    position = lax.broadcasted_iota(jnp.int32, (1, 256), 1).astype(F32)
    mask = jnp.where(position < jnp.concatenate([total, total], axis=1), 1.0, 0.0)

    def step(pair, _):
        lanes = tile_of(pair, 128)
        query = q_ref[:, lanes]
        scores = lax.dot_general(
            split_heads(query), k_ref[:, lanes], NT, preferred_element_type=F32
        )
        raw = jnp.exp(scores) * mask
        prob = (raw / jnp.sum(raw, axis=1, keepdims=True)).astype(BF16)
        p_ref[2 * pair] = prob[:256]
        p_ref[2 * pair + 1] = prob[256:]
        qt_ref[lanes, :] = query.T
        return 0

    lax.fori_loop(0, 16, step, 0)


def relay_attention(rows, arrive, gy_ref, wo_ref, q_ref, k_ref, vt_ref, p_ref, ga_ref, gs_ref, gq_ref, sum_ref, dot_ref):
    for tile in range(TILES):
        arrive(tile)
        cols = slice(tile * TILE, (tile + 1) * TILE)
        grad_y = gy_ref[rows, cols]
        for j in range(2):
            lanes = slice(j * 1024, (j + 1) * 1024)
            weight = wide(wo_ref, range(8 * j, 8 * j + 8), cols)
            part = jnp.dot(grad_y, weight, preferred_element_type=F32)
            if tile:
                part = sum_ref[:, lanes] + part
            if tile < TILES - 1:
                sum_ref[:, lanes] = part
            else:
                ga_ref[rows, lanes] = part.astype(BF16)
    low = low_lanes(CHUNK)
    product = jnp.zeros((CHUNK, 128), F32)
    for pair in range(16):
        lanes = slice(pair * 128, (pair + 1) * 128)
        both = split_heads(ga_ref[rows, lanes])
        grad_prob = jnp.dot(both, vt_ref[lanes, :], preferred_element_type=F32)
        prob = jnp.concatenate([p_ref[2 * pair, rows, :], p_ref[2 * pair + 1, rows, :]], axis=0)
        prob = prob.astype(F32)
        inner = jnp.sum(prob * grad_prob, axis=1, keepdims=True)
        grad_scores = (prob * (grad_prob - inner)).astype(BF16)
        gs_ref[2 * pair, rows, :] = grad_scores[:CHUNK]
        gs_ref[2 * pair + 1, rows, :] = grad_scores[CHUNK:]
        both_query = jnp.dot(grad_scores, k_ref[:, lanes], preferred_element_type=F32)
        grad_query = jnp.where(low, both_query[:CHUNK], both_query[CHUNK:]).astype(BF16)
        gq_ref[:, lanes] = grad_query
        product = product + grad_query.astype(F32) * q_ref[rows, lanes].astype(F32)
    dot_ref[...] = jnp.sum(product, axis=1, keepdims=True) + jnp.zeros((CHUNK, 128), F32)


def relay_output(rows, leave, gy_ref, x_ref, gain_ref, inv_ref, wq_ref, gq_ref, dot_ref, out_ref):
    inv_rms = inv_ref[rows, 0:1]
    x_scale = inv_rms * inv_rms * dot_ref[:, 0:1] * (1.0 / FULL)
    grad_query = gq_ref[...]
    for tile in range(TILES):
        cols = slice(tile * TILE, (tile + 1) * TILE)
        blocks = range(tile * 16 // TILES, (tile + 1) * 16 // TILES)
        grad_normed = jnp.dot(grad_query, wide(wq_ref, blocks), preferred_element_type=F32)
        scaled = grad_normed * gain_ref[:, cols].astype(F32)
        branch = inv_rms * scaled - x_ref[rows, cols].astype(F32) * x_scale
        out_ref[rows, cols] = (gy_ref[rows, cols].astype(F32) + branch).astype(BF16)
        leave(tile)


def key_value_grads(qt_ref, gs_ref, p_ref, ga_ref, gk_ref):
    def step(quad, _):
        for inside in range(4):
            pair = quad * 4 + inside
            lanes = tile_of(pair, 128)
            query_t = qt_ref[lanes, :]
            attn_t = ga_ref[:, lanes].T
            for left, right_ref, out_ref in ((query_t, gs_ref, gk_ref), (attn_t, p_ref, ga_ref)):
                heads = [
                    jnp.dot(
                        left[head * HEAD : (head + 1) * HEAD],
                        right_ref[2 * pair + head],
                        preferred_element_type=F32,
                    )
                    for head in range(2)
                ]
                out_ref[:, lanes] = jnp.concatenate(heads, axis=0).astype(BF16).T
        return 0

    lax.fori_loop(0, 4, step, 0)


def whole_kernel(
    wq_own_ref, wk_own_ref, wo_own_ref, wv_own_ref, enc_own_ref, valid_ref, x_ref, gout_ref, gain_ref,
    gin_ref, genc_ref,
    full_ref, transit_ref, enc_ref, count_own_ref, count_ref, gy_ref, q_ref, qt_ref, k_ref, vt_ref, p_ref, gs_ref, ga_ref,
    gq_ref, sum_ref, dot_ref, inv_ref, acc_ref, slot_ref,
    send_sem, recv_sem, transit_send, transit_recv, local_sem,
    enc_send, enc_recv, count_send, count_recv, relay_send, relay_recv, term_send, term_recv,
):
    sections = lax.axis_size("section")
    section, dp = lax.axis_index("section"), lax.axis_index("dp")
    gather = Gather((wq_own_ref, wk_own_ref, wo_own_ref, wv_own_ref), full_ref, send_sem, recv_sem, transit_ref, transit_send, transit_recv)
    offsets = range(1, sections)

    def other(offset):
        return (section + offset) % sections

    def remote(src, dst, send, recv, to):
        return pltpu.make_async_remote_copy(
            src_ref=src, dst_ref=dst, send_sem=send, recv_sem=recv,
            device_id=(to, dp), device_id_type=MESH,
        )

    barrier = pltpu.get_barrier_semaphore()
    greeted = gather.greet(barrier)
    for offset in offsets:
        pl.semaphore_signal(barrier, inc=1, device_id=(other(offset), dp), device_id_type=MESH)
    gather.turn(0)
    valid = jnp.sum(valid_ref[...].astype(F32), axis=1, keepdims=True)
    count_own_ref[...] = jnp.broadcast_to(valid, count_own_ref.shape)
    helpers = jnp.where(section >= gather.away, 3, 0)
    pl.semaphore_wait(barrier, greeted + len(offsets) + helpers)

    my_rows = tile_of(section, enc_own_ref.shape[0])

    def enc_copies(offset):
        return (
            remote(enc_own_ref, enc_ref.at[my_rows], enc_send.at[offset], enc_recv.at[offset], other(offset)),
            remote(count_own_ref, count_ref.at[section], count_send.at[offset], count_recv.at[offset], other(offset)),
        )

    gather.stage(0, 0)
    gather.turn(1)
    gather.stage(1, 0)
    for offset in offsets:
        for copy in enc_copies(offset):
            copy.start()
    enc_ref[my_rows, :] = enc_own_ref[...]
    count_ref[section] = count_own_ref[...]
    gather.turn(2)
    gather.turn(3)

    @pl.when(section == sections - 1)
    def _():
        pltpu.make_async_copy(gout_ref, gy_ref, local_sem.at[0]).start()

    def norm(chunk, _):
        rows = tile_of(chunk, 32)
        x = x_ref[rows, :].astype(F32)
        inv_rms = inverse_rms(x)
        inv_ref[rows, :] = jnp.broadcast_to(inv_rms, (32, 128))
        gin_ref[rows, :] = (x * inv_rms * gain_ref[...].astype(F32)).astype(BF16)
        return 0

    lax.fori_loop(0, gy_ref.shape[0] // 32, norm, 0)

    def stages(*steps):
        for matrix, number in steps:
            gather.stage(matrix, number)

    gather.help(0)
    stages((0, 1), (0, 2), (2, 0))
    gather.help(1)
    stages((1, 1), (1, 2))
    gather.help(2)
    stages((0, 3), (3, 0))
    gather.help(3)
    stages((2, 1), (2, 2), (1, 3), (0, 4), (0, 5))
    project(gin_ref, full_ref.at[Q], q_ref)
    stages((3, 1), (3, 2), (2, 3), (1, 4), (1, 5))
    for offset in offsets:
        for copy in enc_copies(offset):
            copy.wait_recv()
    project(enc_ref, full_ref.at[K], k_ref)
    probabilities(q_ref, k_ref, count_ref, p_ref, qt_ref)
    stages((3, 3), (2, 4), (3, 4))
    project_values(gather.core, enc_ref, full_ref.at[V], acc_ref, vt_ref, False)
    stages((2, 5), (3, 5))
    project_values(1 - gather.core, enc_ref, full_ref.at[V], acc_ref, vt_ref, True)

    @pl.when(section == sections - 1)
    def _():
        pltpu.make_async_copy(gout_ref, gy_ref, local_sem.at[0]).wait()

    chunks = gy_ref.shape[0] // CHUNK

    def send(chunk, tile):
        rows, cols = tile_of(chunk, CHUNK), pl.ds(tile * TILE, TILE)
        return remote(
            gin_ref.at[rows, cols], gy_ref.at[rows, cols],
            relay_send.at[chunk, tile], relay_recv.at[chunk, tile], other(sections - 1),
        )

    def attention(chunk):
        def arrive(tile):
            @pl.when(section < sections - 1)
            def _():
                send(chunk, tile).wait_recv()

        relay_attention(
            tile_of(chunk, CHUNK), arrive, gy_ref, full_ref.at[O], q_ref, k_ref, vt_ref, p_ref,
            ga_ref, gs_ref, gq_ref, sum_ref, dot_ref,
        )

    def output(chunk, leave):
        relay_output(
            tile_of(chunk, CHUNK), leave, gy_ref, x_ref, gain_ref, inv_ref, full_ref.at[Q],
            gq_ref, dot_ref, gin_ref,
        )

    def step(chunk, _):
        attention(chunk)

        @pl.when(jnp.logical_or(section > 0, chunk < chunks - 1))
        def _():
            def leave(tile):
                @pl.when(section > 0)
                def _():
                    send(chunk, tile).start()

            output(chunk, leave)

        return 0

    lax.fori_loop(0, chunks, step, 0)

    key_value_grads(qt_ref, gs_ref, p_ref, ga_ref, k_ref)
    width = FULL // ENC_TILES
    enc_rows = enc_own_ref.shape[0]

    def term_copy(tile, offset):
        cols = pl.ds(tile * width, width)
        return remote(
            enc_ref.at[tile_of(other(offset), enc_rows), cols], slot_ref.at[offset, :, cols],
            term_send.at[tile, offset], term_recv.at[tile, offset], other(offset),
        )

    for tile in range(ENC_TILES):
        blocks = range(tile * 16 // ENC_TILES, (tile + 1) * 16 // ENC_TILES)
        part = jnp.dot(k_ref[...], wide(full_ref.at[K], blocks), preferred_element_type=F32)
        part = part + jnp.dot(ga_ref[...], wide(full_ref.at[V], blocks), preferred_element_type=F32)
        enc_ref[:, tile * width : (tile + 1) * width] = part.astype(BF16)
        for offset in offsets:
            term_copy(tile, offset).start()

    @pl.when(section == 0)
    def _():
        output(chunks - 1, lambda tile: None)

    for matrix in range(4):
        gather.finish(matrix)
    for offset in offsets:
        for copy in enc_copies(offset):
            copy.wait_send()

    @pl.when(section > 0)
    def _():
        def done(chunk, _):
            for tile in range(TILES):
                send(chunk, tile).wait_send()
            return 0

        lax.fori_loop(0, chunks, done, 0)

    for tile in range(ENC_TILES):
        cols = slice(tile * width, (tile + 1) * width)
        total = enc_ref[my_rows, cols].astype(F32)
        for offset in offsets:
            term_copy(tile, offset).wait_recv()
            total = total + slot_ref[offset, :, cols].astype(F32)
        genc_ref[:, cols] = total.astype(BF16)
    for tile in range(ENC_TILES):
        for offset in offsets:
            term_copy(tile, offset).wait_send()


def whole(shards, enc_own, valid, x, grad_out, gain):
    rows, width = x.shape
    sections = lax.axis_size("section")
    enc_rows = enc_own.shape[0]
    chunks = rows // CHUNK
    vmem = pl.BlockSpec(memory_space=pltpu.VMEM)
    any_space = pl.BlockSpec(memory_space=pl.ANY)
    dma = pltpu.SemaphoreType.DMA
    half = pltpu.VMEM((rows, width), BF16)
    turned = pltpu.VMEM((width, rows), BF16)
    per_head = pltpu.VMEM((width // HEAD, rows, rows), BF16)
    return pl.pallas_call(
        whole_kernel,
        out_shape=(
            jax.ShapeDtypeStruct((rows, width), BF16),
            jax.ShapeDtypeStruct((enc_rows, width), BF16),
        ),
        in_specs=[vmem] * 7 + [any_space, vmem],
        out_specs=(vmem, vmem),
        scratch_shapes=[
            pltpu.VMEM((4, 16, FULL, 128), BF16),
            pltpu.VMEM((4, 3, DETOUR, 128), BF16),
            half,
            pltpu.VMEM((8, 128), F32),
            pltpu.VMEM((sections, 8, 128), F32),
            half,
            half,
            turned,
            half,
            turned,
            per_head,
            per_head,
            half,
            pltpu.VMEM((CHUNK, width), BF16),
            pltpu.VMEM((CHUNK, width), F32),
            pltpu.VMEM((CHUNK, 128), F32),
            pltpu.VMEM((rows, 128), F32),
            pltpu.VMEM((width, rows), F32),
            pltpu.VMEM((sections, enc_rows, width), BF16),
            dma((4, COPIES)),
            dma((4, COPIES)),
            dma((4, 3)),
            dma((4, 3)),
            dma((1,)),
            dma((sections,)),
            dma((sections,)),
            dma((sections,)),
            dma((sections,)),
            dma((chunks, TILES)),
            dma((chunks, TILES)),
            dma((ENC_TILES, sections)),
            dma((ENC_TILES, sections)),
        ],
        compiler_params=pltpu.CompilerParams(
            collective_id=0, has_side_effects=True, vmem_limit_bytes=62 * 2**20
        ),
    )(*shards, enc_own, valid, x, grad_out, gain)


def per_device(
    hidden_in, grad_out, encoder_out, enc_valid, norm_gain, w_query, w_key, w_value, w_out
):
    shards = (w_query[0], w_key[0], w_out[0], w_value[0])
    grad_in, enc_grad = whole(
        shards, encoder_out[0], enc_valid, hidden_in[0, 0], grad_out[0], norm_gain
    )
    return (grad_in[None, None], enc_grad[None])


def solution(mesh):
    in_specs = (
        P("section", "dp", None, None),
        P("dp", None, None),
        P("dp", "section", None),
        P("dp", "section"),
        P("section", None),
        P("section", "dp", None),
        P("section", "dp", None),
        P("section", "dp", None),
        P("section", "dp", None),
    )
    out_specs = (P("section", "dp", None, None), P("dp", "section", None))
    return jax.shard_map(
        per_device, mesh=mesh, in_specs=in_specs, out_specs=out_specs, check_vma=False
    )
```

```python
import functools

import jax
import jax.numpy as jnp
from jax import lax
from jax.experimental import pallas as pl
from jax.experimental.pallas import tpu as pltpu
from jax.sharding import PartitionSpec as P

HEAD = 64
MESH = pl.DeviceIdType.MESH
F32 = jnp.float32
BF16 = jnp.bfloat16

FULL = 2048
HALF = FULL // 2
PART_A = 1280
HALF_A = PART_A // 2
COPIES = 31
DETOUR = 704
CHUNK = 32
TILES = 4
TILE = 2048 // TILES


def copy_plan():
    part_b = FULL - PART_A
    return [
        (0, 0, 0, HALF, "z+"),
        (0, 0, DETOUR, FULL - DETOUR, "z-"),
        (0, 0, 0, PART_A, "y"),
        (0, 0, PART_A + DETOUR, part_b - DETOUR, "y"),
        (0, 0, 0, FULL, "core"),
        (0, -1, 0, HALF, "z+"),
        (0, -1, PART_A, part_b, "y"),
        (0, -1, 0, FULL, "core"),
        (0, 1, HALF, HALF, "z-"),
        (0, 1, PART_A, part_b, "y"),
        (0, 1, 0, FULL, "core"),
        (1, 0, 0, PART_A, "z+"),
        (1, 0, 0, PART_A, "z-"),
        (1, 0, 0, PART_A, "core"),
        (1, 0, PART_A, part_b, "core"),
        (0, 2, 0, HALF, "core"),
        (0, 2, PART_A, part_b, "y"),
        (0, 2, HALF, HALF, "core"),
        (1, -1, 0, HALF_A, "z+"),
        (1, -1, 0, PART_A, "core"),
        (1, 1, HALF_A, HALF_A, "z-"),
        (1, 1, 0, PART_A, "core"),
        (1, -1, PART_A, part_b, "core"),
        (1, 1, PART_A, part_b, "core"),
        (1, 2, 0, HALF_A, "core"),
        (1, 2, HALF_A, HALF_A, "core"),
        (1, 2, PART_A, part_b, "core"),
        (0, 0, HALF, DETOUR, "z+"),
        (0, 0, 0, DETOUR, "z-"),
        (0, 0, PART_A, DETOUR, "y"),
        (0, 0, HALF + DETOUR, HALF - DETOUR, "z+"),
    ]


PLAN = copy_plan()
DETOURS = (27, 28, 29)
STAGES = [
    ((), (27, 28, 29, 0, 1, 2, 3, 30, 4)),
    ((0, 1, 2, 3, 30), (5, 8, 11, 12, 9, 13)),
    ((27, 28, 29), (6, 7, 10, 14)),
    ((5, 8, 11, 12, 9), (18, 20, 16, 15, 17, 19, 21, 23)),
    ((18, 20, 16, 6), (24, 25, 26, 22)),
    ((4, 7, 10, 13, 14, 15, 17, 19, 21, 22, 23, 24, 25, 26), ()),
]


class Gather:
    def __init__(self, shard_refs, full_ref, send_sem, recv_sem, transit_ref, transit_send, transit_recv):
        self.shards, self.full = shard_refs, full_ref
        self.transit_ref, self.transit_send, self.transit_recv = transit_ref, transit_send, transit_recv
        self.send_sem, self.recv_sem = send_sem, recv_sem
        self.section, dp = lax.axis_index("section"), lax.axis_index("dp")
        self.half, self.z, self.core = dp // 8, (dp // 2) % 4, dp % 2

    def dp_of(self, half, z, core):
        return half * 8 + ((z + 4) % 4) * 2 + core

    def target(self, name):
        half, z, core = self.half, self.z, self.core
        dp = {
            "z+": self.dp_of(half, z + 1, core),
            "z-": self.dp_of(half, z + 3, core),
            "y": self.dp_of(1 - half, z, core),
            "core": self.dp_of(half, z, 1 - core),
        }[name]
        return (self.section, dp)

    def greet(self, barrier):
        for name in ("z+", "z-", "y", "core"):
            pl.semaphore_signal(barrier, inc=1, device_id=self.target(name), device_id_type=MESH)
        self.away = lax.axis_size("section") - 2

        @pl.when(self.section < 2)
        def _():
            for name in ("z+", "z-", "y"):
                _, dp = self.target(name)
                pl.semaphore_signal(
                    barrier, inc=1, device_id=(self.section + self.away, dp), device_id_type=MESH
                )

        return 4

    def detour(self, matrix, index):
        k = DETOURS[index]
        _, dp = self.target(PLAN[k][4])
        me = self.dp_of(self.half, self.z, self.core)
        return pltpu.make_async_remote_copy(
            src_ref=self.full.at[matrix, me, pl.ds(PLAN[k][2], DETOUR)],
            dst_ref=self.transit_ref.at[matrix, index],
            send_sem=self.send_sem.at[matrix, k],
            recv_sem=self.transit_recv.at[matrix, index],
            device_id=(self.section - self.away, dp),
            device_id_type=MESH,
        )

    def onward(self, matrix, index):
        half, z, core = self.half, self.z, self.core
        unit = (self.dp_of(half, z + 3, core), self.dp_of(half, z + 1, core), self.dp_of(1 - half, z, core))[index]
        return pltpu.make_async_remote_copy(
            src_ref=self.transit_ref.at[matrix, index],
            dst_ref=self.full.at[matrix, unit, pl.ds(PLAN[DETOURS[index]][2], DETOUR)],
            send_sem=self.transit_send.at[matrix, index],
            recv_sem=self.recv_sem.at[matrix, DETOURS[index]],
            device_id=(self.section + self.away, self.dp_of(half, z, core)),
            device_id_type=MESH,
        )

    def help(self, matrix):
        @pl.when(self.section < 2)
        def _():
            for index in range(3):
                self.detour(matrix, index).wait_recv()
                self.onward(matrix, index).start()

    def turn(self, matrix):
        me = self.dp_of(self.half, self.z, self.core)
        shard = self.shards[matrix]

        def step(quad, _):
            for inside in range(4):
                lanes = tile_of(quad * 4 + inside, 128)
                self.full[matrix, me, lanes, :] = shard[:, lanes].T
            return 0

        lax.fori_loop(0, FULL // 512, step, 0)

    def copy(self, matrix, k):
        half_off, z_off, first, rows, name = PLAN[k]
        half = 1 - self.half if half_off else self.half
        unit = self.dp_of(half, self.z + (z_off + 4) % 4, self.core)
        block = self.full.at[matrix, unit, pl.ds(first, rows)]
        return pltpu.make_async_remote_copy(
            src_ref=block,
            dst_ref=block,
            send_sem=self.send_sem.at[matrix, k],
            recv_sem=self.recv_sem.at[matrix, k],
            device_id=self.target(name),
            device_id_type=MESH,
        )

    def stage(self, matrix, number):
        waits, starts = STAGES[number]
        for k in waits:
            self.copy(matrix, k).wait_recv()
        for k in starts:
            if k in DETOURS:
                @pl.when(self.section >= self.away)
                def _():
                    self.detour(matrix, DETOURS.index(k)).start()

                @pl.when(self.section < self.away)
                def _():
                    self.copy(matrix, k).start()
            else:
                self.copy(matrix, k).start()

    def finish(self, matrix):
        for k in range(COPIES):
            self.copy(matrix, k).wait_send()

        @pl.when(self.section < 2)
        def _():
            for index in range(3):
                self.onward(matrix, index).wait_send()


Q, K, O, V = 0, 1, 2, 3
ENC_TILES = 4
NT = (((1,), (1,)), ((), ()))


def wide(ref, blocks, rows=slice(None)):
    return jnp.concatenate([ref[block, rows, :] for block in blocks], axis=1)


def low_lanes(rows):
    return lax.broadcasted_iota(jnp.int32, (rows, 128), 1) < HEAD


def split_heads(pair):
    low = low_lanes(pair.shape[0])
    zero = jnp.zeros(pair.shape, pair.dtype)
    return jnp.concatenate([jnp.where(low, pair, zero), jnp.where(low, zero, pair)], axis=0)


def inverse_rms(x):
    return lax.rsqrt(jnp.sum(x * x, axis=1, keepdims=True) * (1.0 / x.shape[1]) + 1e-06)


def tile_of(index, size):
    return pl.ds(pl.multiple_of(index * size, size), size)


def project(act_ref, weight_ref, out_ref):
    def tile(index, _):
        rows = tile_of(index, 256)
        weight = wide(weight_ref, range(16), rows)
        part = lax.dot_general(act_ref[...], weight, NT, preferred_element_type=F32)
        out_ref[:, rows] = part.astype(BF16)
        return 0

    lax.fori_loop(0, FULL // 256, tile, 0)


def project_values(core, enc_ref, weight_ref, acc_ref, out_ref, last):
    blocks = [2 * i + core for i in range(8)]

    def tile(index, _):
        rows = tile_of(index, 256)
        weight = wide(weight_ref, blocks, rows)
        act = jnp.concatenate([enc_ref[:, tile_of(block, 128)] for block in blocks], axis=1)
        part = lax.dot_general(weight, act, NT, preferred_element_type=F32)
        if last:
            out_ref[rows, :] = (acc_ref[rows, :] + part).astype(BF16)
        else:
            acc_ref[rows, :] = part
        return 0

    lax.fori_loop(0, FULL // 256, tile, 0)


def probabilities(q_ref, k_ref, count_ref, p_ref, qt_ref):
    total = jnp.sum(count_ref[...], axis=0)[0:1, :]
    position = lax.broadcasted_iota(jnp.int32, (1, 256), 1).astype(F32)
    mask = jnp.where(position < jnp.concatenate([total, total], axis=1), 1.0, 0.0)

    def step(pair, _):
        lanes = tile_of(pair, 128)
        query = q_ref[:, lanes]
        scores = lax.dot_general(
            split_heads(query), k_ref[:, lanes], NT, preferred_element_type=F32
        )
        raw = jnp.exp(scores) * mask
        prob = (raw / jnp.sum(raw, axis=1, keepdims=True)).astype(BF16)
        p_ref[2 * pair] = prob[:256]
        p_ref[2 * pair + 1] = prob[256:]
        qt_ref[lanes, :] = query.T
        return 0

    lax.fori_loop(0, 16, step, 0)


def relay_attention(rows, arrive, gy_ref, wo_ref, q_ref, k_ref, vt_ref, p_ref, ga_ref, gs_ref, gq_ref, sum_ref, dot_ref):
    for tile in range(TILES):
        arrive(tile)
        cols = slice(tile * TILE, (tile + 1) * TILE)
        grad_y = gy_ref[rows, cols]
        for j in range(2):
            lanes = slice(j * 1024, (j + 1) * 1024)
            weight = wide(wo_ref, range(8 * j, 8 * j + 8), cols)
            part = jnp.dot(grad_y, weight, preferred_element_type=F32)
            if tile:
                part = sum_ref[:, lanes] + part
            if tile < TILES - 1:
                sum_ref[:, lanes] = part
            else:
                ga_ref[rows, lanes] = part.astype(BF16)
    low = low_lanes(CHUNK)
    product = jnp.zeros((CHUNK, 128), F32)
    for pair in range(16):
        lanes = slice(pair * 128, (pair + 1) * 128)
        both = split_heads(ga_ref[rows, lanes])
        grad_prob = jnp.dot(both, vt_ref[lanes, :], preferred_element_type=F32)
        prob = jnp.concatenate([p_ref[2 * pair, rows, :], p_ref[2 * pair + 1, rows, :]], axis=0)
        prob = prob.astype(F32)
        inner = jnp.sum(prob * grad_prob, axis=1, keepdims=True)
        grad_scores = (prob * (grad_prob - inner)).astype(BF16)
        gs_ref[2 * pair, rows, :] = grad_scores[:CHUNK]
        gs_ref[2 * pair + 1, rows, :] = grad_scores[CHUNK:]
        both_query = jnp.dot(grad_scores, k_ref[:, lanes], preferred_element_type=F32)
        grad_query = jnp.where(low, both_query[:CHUNK], both_query[CHUNK:]).astype(BF16)
        gq_ref[:, lanes] = grad_query
        product = product + grad_query.astype(F32) * q_ref[rows, lanes].astype(F32)
    dot_ref[...] = jnp.sum(product, axis=1, keepdims=True) + jnp.zeros((CHUNK, 128), F32)


def relay_output(rows, leave, gy_ref, x_ref, gain_ref, inv_ref, wq_ref, gq_ref, dot_ref, out_ref):
    inv_rms = inv_ref[rows, 0:1]
    x_scale = inv_rms * inv_rms * dot_ref[:, 0:1] * (1.0 / FULL)
    grad_query = gq_ref[...]
    for tile in range(TILES):
        cols = slice(tile * TILE, (tile + 1) * TILE)
        blocks = range(tile * 16 // TILES, (tile + 1) * 16 // TILES)
        grad_normed = jnp.dot(grad_query, wide(wq_ref, blocks), preferred_element_type=F32)
        scaled = grad_normed * gain_ref[:, cols].astype(F32)
        branch = inv_rms * scaled - x_ref[rows, cols].astype(F32) * x_scale
        out_ref[rows, cols] = (gy_ref[rows, cols].astype(F32) + branch).astype(BF16)
        leave(tile)


def key_value_grads(qt_ref, gs_ref, p_ref, ga_ref, gk_ref):
    def step(quad, _):
        for inside in range(4):
            pair = quad * 4 + inside
            lanes = slice(pair * 128, (pair + 1) * 128)
            query_t = qt_ref[lanes, :]
            attn_t = ga_ref[:, lanes].T
            for left, right_ref, out_ref in ((query_t, gs_ref, gk_ref), (attn_t, p_ref, ga_ref)):
                heads = [
                    jnp.dot(
                        left[head * HEAD : (head + 1) * HEAD],
                        right_ref[2 * pair + head],
                        preferred_element_type=F32,
                    )
                    for head in range(2)
                ]
                out_ref[:, lanes] = jnp.concatenate(heads, axis=0).astype(BF16).T
        return 0

    for quad in range(4):
        step(quad, 0)


def whole_kernel(
    wq_own_ref, wk_own_ref, wo_own_ref, wv_own_ref, enc_own_ref, valid_ref, x_ref, gout_ref, gain_ref,
    gin_ref, genc_ref,
    full_ref, transit_ref, enc_ref, count_own_ref, count_ref, gy_ref, q_ref, qt_ref, k_ref, vt_ref, p_ref, gs_ref, ga_ref,
    gq_ref, sum_ref, dot_ref, inv_ref, acc_ref, slot_ref,
    send_sem, recv_sem, transit_send, transit_recv, local_sem,
    enc_send, enc_recv, count_send, count_recv, relay_send, relay_recv, term_send, term_recv,
):
    sections = lax.axis_size("section")
    section, dp = lax.axis_index("section"), lax.axis_index("dp")
    gather = Gather((wq_own_ref, wk_own_ref, wo_own_ref, wv_own_ref), full_ref, send_sem, recv_sem, transit_ref, transit_send, transit_recv)
    offsets = range(1, sections)

    def other(offset):
        return (section + offset) % sections

    def remote(src, dst, send, recv, to):
        return pltpu.make_async_remote_copy(
            src_ref=src, dst_ref=dst, send_sem=send, recv_sem=recv,
            device_id=(to, dp), device_id_type=MESH,
        )

    barrier = pltpu.get_barrier_semaphore()
    greeted = gather.greet(barrier)
    for offset in offsets:
        pl.semaphore_signal(barrier, inc=1, device_id=(other(offset), dp), device_id_type=MESH)
    gather.turn(0)
    valid = jnp.sum(valid_ref[...].astype(F32), axis=1, keepdims=True)
    count_own_ref[...] = jnp.broadcast_to(valid, count_own_ref.shape)
    helpers = jnp.where(section >= gather.away, 3, 0)
    pl.semaphore_wait(barrier, greeted + len(offsets) + helpers)

    my_rows = tile_of(section, enc_own_ref.shape[0])

    def enc_copies(offset):
        return (
            remote(enc_own_ref, enc_ref.at[my_rows], enc_send.at[offset], enc_recv.at[offset], other(offset)),
            remote(count_own_ref, count_ref.at[section], count_send.at[offset], count_recv.at[offset], other(offset)),
        )

    gather.stage(0, 0)
    gather.turn(1)
    gather.stage(1, 0)
    for offset in offsets:
        for copy in enc_copies(offset):
            copy.start()
    enc_ref[my_rows, :] = enc_own_ref[...]
    count_ref[section] = count_own_ref[...]
    gather.turn(2)
    gather.turn(3)

    @pl.when(section == sections - 1)
    def _():
        pltpu.make_async_copy(gout_ref, gy_ref, local_sem.at[0]).start()

    def norm(chunk, _):
        rows = tile_of(chunk, 32)
        x = x_ref[rows, :].astype(F32)
        inv_rms = inverse_rms(x)
        inv_ref[rows, :] = jnp.broadcast_to(inv_rms, (32, 128))
        gin_ref[rows, :] = (x * inv_rms * gain_ref[...].astype(F32)).astype(BF16)
        return 0

    lax.fori_loop(0, gy_ref.shape[0] // 32, norm, 0)

    def stages(*steps):
        for matrix, number in steps:
            gather.stage(matrix, number)

    gather.help(0)
    stages((0, 1), (0, 2), (2, 0))
    gather.help(1)
    stages((1, 1), (1, 2))
    gather.help(2)
    stages((0, 3), (3, 0))
    gather.help(3)
    stages((2, 1), (2, 2), (1, 3), (0, 4), (0, 5))
    project(gin_ref, full_ref.at[Q], q_ref)
    stages((3, 1), (3, 2), (2, 3), (1, 4), (1, 5))
    for offset in offsets:
        for copy in enc_copies(offset):
            copy.wait_recv()
    project(enc_ref, full_ref.at[K], k_ref)
    probabilities(q_ref, k_ref, count_ref, p_ref, qt_ref)
    stages((3, 3), (2, 4), (3, 4))
    project_values(gather.core, enc_ref, full_ref.at[V], acc_ref, vt_ref, False)
    stages((2, 5), (3, 5))
    project_values(1 - gather.core, enc_ref, full_ref.at[V], acc_ref, vt_ref, True)

    @pl.when(section == sections - 1)
    def _():
        pltpu.make_async_copy(gout_ref, gy_ref, local_sem.at[0]).wait()

    chunks = gy_ref.shape[0] // CHUNK

    def send(chunk, tile):
        rows, cols = tile_of(chunk, CHUNK), pl.ds(tile * TILE, TILE)
        return remote(
            gin_ref.at[rows, cols], gy_ref.at[rows, cols],
            relay_send.at[chunk, tile], relay_recv.at[chunk, tile], other(sections - 1),
        )

    def attention(chunk, has_source):
        def arrive(tile):
            if has_source:
                send(chunk, tile).wait_recv()

        relay_attention(
            tile_of(chunk, CHUNK), arrive, gy_ref, full_ref.at[O], q_ref, k_ref, vt_ref, p_ref,
            ga_ref, gs_ref, gq_ref, sum_ref, dot_ref,
        )

    def output(chunk, has_target):
        def leave(tile):
            if has_target:
                send(chunk, tile).start()

        relay_output(
            tile_of(chunk, CHUNK), leave, gy_ref, x_ref, gain_ref, inv_ref, full_ref.at[Q],
            gq_ref, dot_ref, gin_ref,
        )

    def relay(has_source, has_target):
        def step(chunk, _):
            attention(chunk, has_source)
            output(chunk, has_target)
            return 0

        lax.fori_loop(0, chunks if has_target else chunks - 1, step, 0)

    @pl.when(section == sections - 1)
    def _():
        relay(False, True)

    @pl.when(jnp.logical_and(section > 0, section < sections - 1))
    def _():
        relay(True, True)

    @pl.when(section == 0)
    def _():
        relay(True, False)
        attention(chunks - 1, True)

    key_value_grads(qt_ref, gs_ref, p_ref, ga_ref, k_ref)
    width = FULL // ENC_TILES
    enc_rows = enc_own_ref.shape[0]

    def term_copy(tile, offset):
        cols = pl.ds(tile * width, width)
        return remote(
            enc_ref.at[tile_of(other(offset), enc_rows), cols], slot_ref.at[offset, :, cols],
            term_send.at[tile, offset], term_recv.at[tile, offset], other(offset),
        )

    for tile in range(ENC_TILES):
        blocks = range(tile * 16 // ENC_TILES, (tile + 1) * 16 // ENC_TILES)
        part = jnp.dot(k_ref[...], wide(full_ref.at[K], blocks), preferred_element_type=F32)
        part = part + jnp.dot(ga_ref[...], wide(full_ref.at[V], blocks), preferred_element_type=F32)
        enc_ref[:, tile * width : (tile + 1) * width] = part.astype(BF16)
        for offset in offsets:
            term_copy(tile, offset).start()

    @pl.when(section == 0)
    def _():
        output(chunks - 1, False)

    for matrix in range(4):
        gather.finish(matrix)
    for offset in offsets:
        for copy in enc_copies(offset):
            copy.wait_send()

    @pl.when(section > 0)
    def _():
        def done(chunk, _):
            for tile in range(TILES):
                send(chunk, tile).wait_send()
            return 0

        lax.fori_loop(0, chunks, done, 0)

    for tile in range(ENC_TILES):
        cols = slice(tile * width, (tile + 1) * width)
        total = enc_ref[my_rows, cols].astype(F32)
        for offset in offsets:
            term_copy(tile, offset).wait_recv()
            total = total + slot_ref[offset, :, cols].astype(F32)
        genc_ref[:, cols] = total.astype(BF16)
    for tile in range(ENC_TILES):
        for offset in offsets:
            term_copy(tile, offset).wait_send()


def whole(shards, enc_own, valid, x, grad_out, gain):
    rows, width = x.shape
    sections = lax.axis_size("section")
    enc_rows = enc_own.shape[0]
    chunks = rows // CHUNK
    vmem = pl.BlockSpec(memory_space=pltpu.VMEM)
    any_space = pl.BlockSpec(memory_space=pl.ANY)
    dma = pltpu.SemaphoreType.DMA
    half = pltpu.VMEM((rows, width), BF16)
    turned = pltpu.VMEM((width, rows), BF16)
    per_head = pltpu.VMEM((width // HEAD, rows, rows), BF16)
    return pl.pallas_call(
        whole_kernel,
        out_shape=(
            jax.ShapeDtypeStruct((rows, width), BF16),
            jax.ShapeDtypeStruct((enc_rows, width), BF16),
        ),
        in_specs=[vmem] * 7 + [any_space, vmem],
        out_specs=(vmem, vmem),
        scratch_shapes=[
            pltpu.VMEM((4, 16, FULL, 128), BF16),
            pltpu.VMEM((4, 3, DETOUR, 128), BF16),
            half,
            pltpu.VMEM((8, 128), F32),
            pltpu.VMEM((sections, 8, 128), F32),
            half,
            half,
            turned,
            half,
            turned,
            per_head,
            per_head,
            half,
            pltpu.VMEM((CHUNK, width), BF16),
            pltpu.VMEM((CHUNK, width), F32),
            pltpu.VMEM((CHUNK, 128), F32),
            pltpu.VMEM((rows, 128), F32),
            pltpu.VMEM((width, rows), F32),
            pltpu.VMEM((sections, enc_rows, width), BF16),
            dma((4, COPIES)),
            dma((4, COPIES)),
            dma((4, 3)),
            dma((4, 3)),
            dma((1,)),
            dma((sections,)),
            dma((sections,)),
            dma((sections,)),
            dma((sections,)),
            dma((chunks, TILES)),
            dma((chunks, TILES)),
            dma((ENC_TILES, sections)),
            dma((ENC_TILES, sections)),
        ],
        compiler_params=pltpu.CompilerParams(
            collective_id=0, has_side_effects=True, vmem_limit_bytes=62 * 2**20
        ),
    )(*shards, enc_own, valid, x, grad_out, gain)


def per_device(
    hidden_in, grad_out, encoder_out, enc_valid, norm_gain, w_query, w_key, w_value, w_out
):
    shards = (w_query[0], w_key[0], w_out[0], w_value[0])
    grad_in, enc_grad = whole(
        shards, encoder_out[0], enc_valid, hidden_in[0, 0], grad_out[0], norm_gain
    )
    return (grad_in[None, None], enc_grad[None])


def solution(mesh):
    in_specs = (
        P("section", "dp", None, None),
        P("dp", None, None),
        P("dp", "section", None),
        P("dp", "section"),
        P("section", None),
        P("section", "dp", None),
        P("section", "dp", None),
        P("section", "dp", None),
        P("section", "dp", None),
    )
    out_specs = (P("section", "dp", None, None), P("dp", "section", None))
    return jax.shard_map(
        per_device, mesh=mesh, in_specs=in_specs, out_specs=out_specs, check_vma=False
    )
```

```python
import functools

import jax
import jax.numpy as jnp
from jax import lax
from jax.experimental import pallas as pl
from jax.experimental.pallas import tpu as pltpu
from jax.sharding import PartitionSpec as P

HEAD = 64
MESH = pl.DeviceIdType.MESH
F32 = jnp.float32
BF16 = jnp.bfloat16

FULL = 2048
HALF = FULL // 2
PART_A = 1280
HALF_A = PART_A // 2
COPIES = 31
DETOUR = 704
CHUNK = 32
TILES = 4
TILE = 2048 // TILES


def copy_plan():
    part_b = FULL - PART_A
    return [
        (0, 0, 0, HALF, "z+"),
        (0, 0, DETOUR, FULL - DETOUR, "z-"),
        (0, 0, 0, PART_A, "y"),
        (0, 0, PART_A + DETOUR, part_b - DETOUR, "y"),
        (0, 0, 0, FULL, "core"),
        (0, -1, 0, HALF, "z+"),
        (0, -1, PART_A, part_b, "y"),
        (0, -1, 0, FULL, "core"),
        (0, 1, HALF, HALF, "z-"),
        (0, 1, PART_A, part_b, "y"),
        (0, 1, 0, FULL, "core"),
        (1, 0, 0, PART_A, "z+"),
        (1, 0, 0, PART_A, "z-"),
        (1, 0, 0, PART_A, "core"),
        (1, 0, PART_A, part_b, "core"),
        (0, 2, 0, HALF, "core"),
        (0, 2, PART_A, part_b, "y"),
        (0, 2, HALF, HALF, "core"),
        (1, -1, 0, HALF_A, "z+"),
        (1, -1, 0, PART_A, "core"),
        (1, 1, HALF_A, HALF_A, "z-"),
        (1, 1, 0, PART_A, "core"),
        (1, -1, PART_A, part_b, "core"),
        (1, 1, PART_A, part_b, "core"),
        (1, 2, 0, HALF_A, "core"),
        (1, 2, HALF_A, HALF_A, "core"),
        (1, 2, PART_A, part_b, "core"),
        (0, 0, HALF, DETOUR, "z+"),
        (0, 0, 0, DETOUR, "z-"),
        (0, 0, PART_A, DETOUR, "y"),
        (0, 0, HALF + DETOUR, HALF - DETOUR, "z+"),
    ]


PLAN = copy_plan()
DETOURS = (27, 28, 29)
STAGES = [
    ((), (27, 28, 29, 0, 1, 2, 3, 30, 4)),
    ((0, 1, 2, 3, 30), (5, 8, 11, 12, 9, 13)),
    ((27, 28, 29), (6, 7, 10, 14)),
    ((5, 8, 11, 12, 9), (18, 20, 16, 15, 17, 19, 21, 23)),
    ((18, 20, 16, 6), (24, 25, 26, 22)),
    ((4, 7, 10, 13, 14, 15, 17, 19, 21, 22, 23, 24, 25, 26), ()),
]


class Gather:
    def __init__(self, shard_refs, full_ref, send_sem, recv_sem, transit_ref, transit_send, transit_recv):
        self.shards, self.full = shard_refs, full_ref
        self.transit_ref, self.transit_send, self.transit_recv = transit_ref, transit_send, transit_recv
        self.send_sem, self.recv_sem = send_sem, recv_sem
        self.section, dp = lax.axis_index("section"), lax.axis_index("dp")
        self.half, self.z, self.core = dp // 8, (dp // 2) % 4, dp % 2

    def dp_of(self, half, z, core):
        return half * 8 + ((z + 4) % 4) * 2 + core

    def target(self, name):
        half, z, core = self.half, self.z, self.core
        dp = {
            "z+": self.dp_of(half, z + 1, core),
            "z-": self.dp_of(half, z + 3, core),
            "y": self.dp_of(1 - half, z, core),
            "core": self.dp_of(half, z, 1 - core),
        }[name]
        return (self.section, dp)

    def greet(self, barrier):
        for name in ("z+", "z-", "y", "core"):
            pl.semaphore_signal(barrier, inc=1, device_id=self.target(name), device_id_type=MESH)
        self.away = lax.axis_size("section") - 2

        @pl.when(self.section < 2)
        def _():
            for name in ("z+", "z-", "y"):
                _, dp = self.target(name)
                pl.semaphore_signal(
                    barrier, inc=1, device_id=(self.section + self.away, dp), device_id_type=MESH
                )

        return 4

    def detour(self, matrix, index):
        k = DETOURS[index]
        _, dp = self.target(PLAN[k][4])
        me = self.dp_of(self.half, self.z, self.core)
        return pltpu.make_async_remote_copy(
            src_ref=self.full.at[matrix, me, pl.ds(PLAN[k][2], DETOUR)],
            dst_ref=self.transit_ref.at[matrix, index],
            send_sem=self.send_sem.at[matrix, k],
            recv_sem=self.transit_recv.at[matrix, index],
            device_id=(self.section - self.away, dp),
            device_id_type=MESH,
        )

    def onward(self, matrix, index):
        half, z, core = self.half, self.z, self.core
        unit = (self.dp_of(half, z + 3, core), self.dp_of(half, z + 1, core), self.dp_of(1 - half, z, core))[index]
        return pltpu.make_async_remote_copy(
            src_ref=self.transit_ref.at[matrix, index],
            dst_ref=self.full.at[matrix, unit, pl.ds(PLAN[DETOURS[index]][2], DETOUR)],
            send_sem=self.transit_send.at[matrix, index],
            recv_sem=self.recv_sem.at[matrix, DETOURS[index]],
            device_id=(self.section + self.away, self.dp_of(half, z, core)),
            device_id_type=MESH,
        )

    def help(self, matrix):
        @pl.when(self.section < 2)
        def _():
            for index in range(3):
                self.detour(matrix, index).wait_recv()
                self.onward(matrix, index).start()

    def turn(self, matrix):
        me = self.dp_of(self.half, self.z, self.core)
        shard = self.shards[matrix]

        def step(quad, _):
            for inside in range(4):
                lanes = tile_of(quad * 4 + inside, 128)
                self.full[matrix, me, lanes, :] = shard[:, lanes].T
            return 0

        lax.fori_loop(0, FULL // 512, step, 0)

    def copy(self, matrix, k):
        half_off, z_off, first, rows, name = PLAN[k]
        half = 1 - self.half if half_off else self.half
        unit = self.dp_of(half, self.z + (z_off + 4) % 4, self.core)
        block = self.full.at[matrix, unit, pl.ds(first, rows)]
        return pltpu.make_async_remote_copy(
            src_ref=block,
            dst_ref=block,
            send_sem=self.send_sem.at[matrix, k],
            recv_sem=self.recv_sem.at[matrix, k],
            device_id=self.target(name),
            device_id_type=MESH,
        )

    def stage(self, matrix, number):
        waits, starts = STAGES[number]
        for k in waits:
            self.copy(matrix, k).wait_recv()
        for k in starts:
            if k in DETOURS:
                @pl.when(self.section >= self.away)
                def _():
                    self.detour(matrix, DETOURS.index(k)).start()

                @pl.when(self.section < self.away)
                def _():
                    self.copy(matrix, k).start()
            else:
                self.copy(matrix, k).start()

    def finish(self, matrix):
        for k in range(COPIES):
            self.copy(matrix, k).wait_send()

        @pl.when(self.section < 2)
        def _():
            for index in range(3):
                self.onward(matrix, index).wait_send()


Q, K, O, V = 0, 1, 2, 3
ENC_TILES = 4
NT = (((1,), (1,)), ((), ()))


def wide(ref, blocks, rows=slice(None)):
    return jnp.concatenate([ref[block, rows, :] for block in blocks], axis=1)


def low_lanes(rows):
    return lax.broadcasted_iota(jnp.int32, (rows, 128), 1) < HEAD


def split_heads(pair):
    low = low_lanes(pair.shape[0])
    zero = jnp.zeros(pair.shape, pair.dtype)
    return jnp.concatenate([jnp.where(low, pair, zero), jnp.where(low, zero, pair)], axis=0)


def inverse_rms(x):
    return lax.rsqrt(jnp.sum(x * x, axis=1, keepdims=True) * (1.0 / x.shape[1]) + 1e-06)


def tile_of(index, size):
    return pl.ds(pl.multiple_of(index * size, size), size)


def project(act_ref, weight_ref, out_ref):
    def tile(index, _):
        rows = tile_of(index, 256)
        weight = wide(weight_ref, range(16), rows)
        part = lax.dot_general(act_ref[...], weight, NT, preferred_element_type=F32)
        out_ref[:, rows] = part.astype(BF16)
        return 0

    lax.fori_loop(0, FULL // 256, tile, 0)


def project_values(core, enc_ref, weight_ref, acc_ref, out_ref, last):
    blocks = [2 * i + core for i in range(8)]
    act = jnp.concatenate([enc_ref[:, tile_of(block, 128)] for block in blocks], axis=1)
    for index in range(FULL // 512):
        rows = slice(index * 512, (index + 1) * 512)
        weight = wide(weight_ref, blocks, rows)
        part = lax.dot_general(weight, act, NT, preferred_element_type=F32)
        if last:
            out_ref[rows, :] = (acc_ref[rows, :] + part).astype(BF16)
        else:
            acc_ref[rows, :] = part


def probabilities(q_ref, k_ref, count_ref, p_ref, qt_ref):
    total = jnp.sum(count_ref[...], axis=0)[0:1, :]
    position = lax.broadcasted_iota(jnp.int32, (1, 256), 1).astype(F32)
    mask = jnp.where(position < jnp.concatenate([total, total], axis=1), 1.0, 0.0)

    def step(pair, _):
        lanes = tile_of(pair, 128)
        query = q_ref[:, lanes]
        scores = lax.dot_general(
            split_heads(query), k_ref[:, lanes], NT, preferred_element_type=F32
        )
        raw = jnp.exp(scores) * mask
        prob = (raw / jnp.sum(raw, axis=1, keepdims=True)).astype(BF16)
        p_ref[2 * pair] = prob[:256]
        p_ref[2 * pair + 1] = prob[256:]
        qt_ref[lanes, :] = query.T
        return 0

    lax.fori_loop(0, 16, step, 0)


def relay_attention(rows, arrive, gy_ref, wo_ref, q_ref, k_ref, vt_ref, p_ref, ga_ref, gs_ref, gq_ref, sum_ref, dot_ref):
    for tile in range(TILES):
        arrive(tile)
        cols = slice(tile * TILE, (tile + 1) * TILE)
        grad_y = gy_ref[rows, cols]
        for j in range(2):
            lanes = slice(j * 1024, (j + 1) * 1024)
            weight = wide(wo_ref, range(8 * j, 8 * j + 8), cols)
            part = jnp.dot(grad_y, weight, preferred_element_type=F32)
            if tile:
                part = sum_ref[:, lanes] + part
            if tile < TILES - 1:
                sum_ref[:, lanes] = part
            else:
                ga_ref[rows, lanes] = part.astype(BF16)
    low = low_lanes(CHUNK)
    product = jnp.zeros((CHUNK, 128), F32)
    for pair in range(16):
        lanes = slice(pair * 128, (pair + 1) * 128)
        both = split_heads(ga_ref[rows, lanes])
        grad_prob = jnp.dot(both, vt_ref[lanes, :], preferred_element_type=F32)
        prob = jnp.concatenate([p_ref[2 * pair, rows, :], p_ref[2 * pair + 1, rows, :]], axis=0)
        prob = prob.astype(F32)
        inner = jnp.sum(prob * grad_prob, axis=1, keepdims=True)
        grad_scores = (prob * (grad_prob - inner)).astype(BF16)
        gs_ref[2 * pair, rows, :] = grad_scores[:CHUNK]
        gs_ref[2 * pair + 1, rows, :] = grad_scores[CHUNK:]
        both_query = jnp.dot(grad_scores, k_ref[:, lanes], preferred_element_type=F32)
        grad_query = jnp.where(low, both_query[:CHUNK], both_query[CHUNK:]).astype(BF16)
        gq_ref[:, lanes] = grad_query
        product = product + grad_query.astype(F32) * q_ref[rows, lanes].astype(F32)
    dot_ref[...] = jnp.sum(product, axis=1, keepdims=True) + jnp.zeros((CHUNK, 128), F32)


def relay_output(rows, leave, gy_ref, x_ref, gain_ref, inv_ref, wq_ref, gq_ref, dot_ref, out_ref):
    inv_rms = inv_ref[rows, 0:1]
    x_scale = inv_rms * inv_rms * dot_ref[:, 0:1] * (1.0 / FULL)
    grad_query = gq_ref[...]
    for tile in range(TILES):
        cols = slice(tile * TILE, (tile + 1) * TILE)
        blocks = range(tile * 16 // TILES, (tile + 1) * 16 // TILES)
        grad_normed = jnp.dot(grad_query, wide(wq_ref, blocks), preferred_element_type=F32)
        scaled = grad_normed * gain_ref[:, cols].astype(F32)
        branch = inv_rms * scaled - x_ref[rows, cols].astype(F32) * x_scale
        out_ref[rows, cols] = (gy_ref[rows, cols].astype(F32) + branch).astype(BF16)
        leave(tile)


def key_value_grads(qt_ref, gs_ref, p_ref, ga_ref, gk_ref):
    def step(quad, _):
        for inside in range(4):
            pair = quad * 4 + inside
            lanes = slice(pair * 128, (pair + 1) * 128)
            query_t = qt_ref[lanes, :]
            attn_t = ga_ref[:, lanes].T
            for left, right_ref, out_ref in ((query_t, gs_ref, gk_ref), (attn_t, p_ref, ga_ref)):
                heads = [
                    jnp.dot(
                        left[head * HEAD : (head + 1) * HEAD],
                        right_ref[2 * pair + head],
                        preferred_element_type=F32,
                    )
                    for head in range(2)
                ]
                out_ref[:, lanes] = jnp.concatenate(heads, axis=0).astype(BF16).T
        return 0

    for quad in range(4):
        step(quad, 0)


def whole_kernel(
    wq_own_ref, wk_own_ref, wo_own_ref, wv_own_ref, enc_own_ref, valid_ref, x_ref, gout_ref, gain_ref,
    gin_ref, genc_ref,
    full_ref, transit_ref, enc_ref, count_own_ref, count_ref, gy_ref, q_ref, qt_ref, k_ref, vt_ref, p_ref, gs_ref, ga_ref,
    gq_ref, sum_ref, dot_ref, inv_ref, acc_ref, slot_ref,
    send_sem, recv_sem, transit_send, transit_recv, local_sem,
    enc_send, enc_recv, count_send, count_recv, relay_send, relay_recv, term_send, term_recv,
):
    sections = lax.axis_size("section")
    section, dp = lax.axis_index("section"), lax.axis_index("dp")
    gather = Gather((wq_own_ref, wk_own_ref, wo_own_ref, wv_own_ref), full_ref, send_sem, recv_sem, transit_ref, transit_send, transit_recv)
    offsets = range(1, sections)

    def other(offset):
        return (section + offset) % sections

    def remote(src, dst, send, recv, to):
        return pltpu.make_async_remote_copy(
            src_ref=src, dst_ref=dst, send_sem=send, recv_sem=recv,
            device_id=(to, dp), device_id_type=MESH,
        )

    barrier = pltpu.get_barrier_semaphore()
    greeted = gather.greet(barrier)
    for offset in offsets:
        pl.semaphore_signal(barrier, inc=1, device_id=(other(offset), dp), device_id_type=MESH)
    gather.turn(0)
    valid = jnp.sum(valid_ref[...].astype(F32), axis=1, keepdims=True)
    count_own_ref[...] = jnp.broadcast_to(valid, count_own_ref.shape)
    helpers = jnp.where(section >= gather.away, 3, 0)
    pl.semaphore_wait(barrier, greeted + len(offsets) + helpers)

    my_rows = tile_of(section, enc_own_ref.shape[0])

    def enc_copies(offset):
        return (
            remote(enc_own_ref, enc_ref.at[my_rows], enc_send.at[offset], enc_recv.at[offset], other(offset)),
            remote(count_own_ref, count_ref.at[section], count_send.at[offset], count_recv.at[offset], other(offset)),
        )

    gather.stage(0, 0)
    gather.turn(1)
    gather.stage(1, 0)
    for offset in offsets:
        for copy in enc_copies(offset):
            copy.start()
    enc_ref[my_rows, :] = enc_own_ref[...]
    count_ref[section] = count_own_ref[...]
    gather.turn(2)
    gather.turn(3)

    @pl.when(section == sections - 1)
    def _():
        pltpu.make_async_copy(gout_ref, gy_ref, local_sem.at[0]).start()

    def norm(chunk, _):
        rows = tile_of(chunk, 32)
        x = x_ref[rows, :].astype(F32)
        inv_rms = inverse_rms(x)
        inv_ref[rows, :] = jnp.broadcast_to(inv_rms, (32, 128))
        gin_ref[rows, :] = (x * inv_rms * gain_ref[...].astype(F32)).astype(BF16)
        return 0

    lax.fori_loop(0, gy_ref.shape[0] // 32, norm, 0)

    def stages(*steps):
        for matrix, number in steps:
            gather.stage(matrix, number)

    gather.help(0)
    stages((0, 1), (0, 2), (2, 0))
    gather.help(1)
    stages((1, 1), (1, 2))
    gather.help(2)
    stages((0, 3), (3, 0))
    gather.help(3)
    stages((2, 1), (2, 2), (1, 3), (0, 4), (0, 5))
    project(gin_ref, full_ref.at[Q], q_ref)
    stages((3, 1), (3, 2), (2, 3), (1, 4), (1, 5))
    for offset in offsets:
        for copy in enc_copies(offset):
            copy.wait_recv()
    project(enc_ref, full_ref.at[K], k_ref)
    probabilities(q_ref, k_ref, count_ref, p_ref, qt_ref)
    stages((3, 3), (2, 4), (3, 4))
    project_values(gather.core, enc_ref, full_ref.at[V], acc_ref, vt_ref, False)
    stages((2, 5), (3, 5))
    project_values(1 - gather.core, enc_ref, full_ref.at[V], acc_ref, vt_ref, True)

    @pl.when(section == sections - 1)
    def _():
        pltpu.make_async_copy(gout_ref, gy_ref, local_sem.at[0]).wait()

    chunks = gy_ref.shape[0] // CHUNK

    def send(chunk, tile):
        rows, cols = tile_of(chunk, CHUNK), pl.ds(tile * TILE, TILE)
        return remote(
            gin_ref.at[rows, cols], gy_ref.at[rows, cols],
            relay_send.at[chunk, tile], relay_recv.at[chunk, tile], other(sections - 1),
        )

    def attention(chunk, has_source):
        def arrive(tile):
            if has_source:
                send(chunk, tile).wait_recv()

        relay_attention(
            tile_of(chunk, CHUNK), arrive, gy_ref, full_ref.at[O], q_ref, k_ref, vt_ref, p_ref,
            ga_ref, gs_ref, gq_ref, sum_ref, dot_ref,
        )

    def output(chunk, has_target):
        def leave(tile):
            if has_target:
                send(chunk, tile).start()

        relay_output(
            tile_of(chunk, CHUNK), leave, gy_ref, x_ref, gain_ref, inv_ref, full_ref.at[Q],
            gq_ref, dot_ref, gin_ref,
        )

    def relay(has_source, has_target):
        def step(chunk, _):
            attention(chunk, has_source)
            output(chunk, has_target)
            return 0

        lax.fori_loop(0, chunks if has_target else chunks - 1, step, 0)

    @pl.when(section == sections - 1)
    def _():
        relay(False, True)

    @pl.when(jnp.logical_and(section > 0, section < sections - 1))
    def _():
        relay(True, True)

    @pl.when(section == 0)
    def _():
        relay(True, False)
        attention(chunks - 1, True)

    key_value_grads(qt_ref, gs_ref, p_ref, ga_ref, k_ref)
    width = FULL // ENC_TILES
    enc_rows = enc_own_ref.shape[0]

    def term_copy(tile, offset):
        cols = pl.ds(tile * width, width)
        return remote(
            enc_ref.at[tile_of(other(offset), enc_rows), cols], slot_ref.at[offset, :, cols],
            term_send.at[tile, offset], term_recv.at[tile, offset], other(offset),
        )

    for tile in range(ENC_TILES):
        blocks = range(tile * 16 // ENC_TILES, (tile + 1) * 16 // ENC_TILES)
        part = jnp.dot(k_ref[...], wide(full_ref.at[K], blocks), preferred_element_type=F32)
        part = part + jnp.dot(ga_ref[...], wide(full_ref.at[V], blocks), preferred_element_type=F32)
        enc_ref[:, tile * width : (tile + 1) * width] = part.astype(BF16)
        for offset in offsets:
            term_copy(tile, offset).start()

    @pl.when(section == 0)
    def _():
        output(chunks - 1, False)

    for matrix in range(4):
        gather.finish(matrix)
    for offset in offsets:
        for copy in enc_copies(offset):
            copy.wait_send()

    @pl.when(section > 0)
    def _():
        def done(chunk, _):
            for tile in range(TILES):
                send(chunk, tile).wait_send()
            return 0

        lax.fori_loop(0, chunks, done, 0)

    for tile in range(ENC_TILES):
        cols = slice(tile * width, (tile + 1) * width)
        total = enc_ref[my_rows, cols].astype(F32)
        for offset in offsets:
            term_copy(tile, offset).wait_recv()
            total = total + slot_ref[offset, :, cols].astype(F32)
        genc_ref[:, cols] = total.astype(BF16)
    for tile in range(ENC_TILES):
        for offset in offsets:
            term_copy(tile, offset).wait_send()


def whole(shards, enc_own, valid, x, grad_out, gain):
    rows, width = x.shape
    sections = lax.axis_size("section")
    enc_rows = enc_own.shape[0]
    chunks = rows // CHUNK
    vmem = pl.BlockSpec(memory_space=pltpu.VMEM)
    any_space = pl.BlockSpec(memory_space=pl.ANY)
    dma = pltpu.SemaphoreType.DMA
    half = pltpu.VMEM((rows, width), BF16)
    turned = pltpu.VMEM((width, rows), BF16)
    per_head = pltpu.VMEM((width // HEAD, rows, rows), BF16)
    return pl.pallas_call(
        whole_kernel,
        out_shape=(
            jax.ShapeDtypeStruct((rows, width), BF16),
            jax.ShapeDtypeStruct((enc_rows, width), BF16),
        ),
        in_specs=[vmem] * 7 + [any_space, vmem],
        out_specs=(vmem, vmem),
        scratch_shapes=[
            pltpu.VMEM((4, 16, FULL, 128), BF16),
            pltpu.VMEM((4, 3, DETOUR, 128), BF16),
            half,
            pltpu.VMEM((8, 128), F32),
            pltpu.VMEM((sections, 8, 128), F32),
            half,
            half,
            turned,
            half,
            turned,
            per_head,
            per_head,
            half,
            pltpu.VMEM((CHUNK, width), BF16),
            pltpu.VMEM((CHUNK, width), F32),
            pltpu.VMEM((CHUNK, 128), F32),
            pltpu.VMEM((rows, 128), F32),
            pltpu.VMEM((width, rows), F32),
            pltpu.VMEM((sections, enc_rows, width), BF16),
            dma((4, COPIES)),
            dma((4, COPIES)),
            dma((4, 3)),
            dma((4, 3)),
            dma((1,)),
            dma((sections,)),
            dma((sections,)),
            dma((sections,)),
            dma((sections,)),
            dma((chunks, TILES)),
            dma((chunks, TILES)),
            dma((ENC_TILES, sections)),
            dma((ENC_TILES, sections)),
        ],
        compiler_params=pltpu.CompilerParams(
            collective_id=0, has_side_effects=True, vmem_limit_bytes=62 * 2**20
        ),
    )(*shards, enc_own, valid, x, grad_out, gain)


def per_device(
    hidden_in, grad_out, encoder_out, enc_valid, norm_gain, w_query, w_key, w_value, w_out
):
    shards = (w_query[0], w_key[0], w_out[0], w_value[0])
    grad_in, enc_grad = whole(
        shards, encoder_out[0], enc_valid, hidden_in[0, 0], grad_out[0], norm_gain
    )
    return (grad_in[None, None], enc_grad[None])


def solution(mesh):
    in_specs = (
        P("section", "dp", None, None),
        P("dp", None, None),
        P("dp", "section", None),
        P("dp", "section"),
        P("section", None),
        P("section", "dp", None),
        P("section", "dp", None),
        P("section", "dp", None),
        P("section", "dp", None),
    )
    out_specs = (P("section", "dp", None, None), P("dp", "section", None))
    return jax.shard_map(
        per_device, mesh=mesh, in_specs=in_specs, out_specs=out_specs, check_vma=False
    )
```
